128 devices in a mesh: dp: 16 (over z_lo, x, core), mp: 8 (over y, z_hi).
Axes of the slice: x: 4, y: 4, z: 4 (z_hi: 2, z_lo: 2; z = z_hi * 2 + z_lo), core: 2. Of those that a mesh axis runs over, the one named last changes fastest.
Arguments:
- tokens: bfloat16 [16384, 2048], P(('dp', 'mp')), may hold values from -6 to 6
- segments: int32 [16, 1024], P('dp'), may hold values from 0 to 7, as said below
- norm_gain: bfloat16 [2048], P('dp'), may hold values from 0.3984375 to 1.59375
- norm_shift: bfloat16 [2048], P('dp'), may hold values from -3.5 to 3.5
- qkv_weight: bfloat16 [2048, 3, 2048], P('dp', None, 'mp'), may hold values from -0.125 to 0.125
- qkv_bias: bfloat16 [3, 32, 64], P(None, 'mp', 'dp'), may hold values from -3 to 3
- up_weight: bfloat16 [2048, 8192], P('dp', 'mp'), may hold values from -0.125 to 0.125
- up_bias: bfloat16 [128, 64], P('mp', 'dp'), may hold values from -6 to 6
- out_weight: bfloat16 [2048, 2048], P('mp', 'dp'), may hold values from -2 to 2
- down_weight: bfloat16 [8192, 2048], P('mp', 'dp'), may hold values from -0.0625 to 0.0625
- out_bias: bfloat16 [2048], P('dp'), may hold values from -6 to 6
- cotangent: bfloat16 [16384, 2048], P(('dp', 'mp')), may hold values from -12 to 12
Outputs:
- outputs: bfloat16 [16384, 2048], P(('dp', 'mp'))
- input_grad: bfloat16 [16384, 2048], P(('dp', 'mp'))
- gain_grad: float32 [2048], P(('dp', 'mp'))
- shift_grad: float32 [2048], P(('dp', 'mp'))
- qkv_weight_grad: float32 [2048, 3, 2048], P('dp', None, 'mp')
- qkv_bias_grad: float32 [3, 32, 64], P(None, 'mp', 'dp')
- up_weight_grad: float32 [2048, 8192], P('dp', 'mp')
- up_bias_grad: float32 [128, 64], P('mp', 'dp')
- out_weight_grad: float32 [2048, 2048], P('mp', 'dp')
- down_weight_grad: float32 [8192, 2048], P('mp', 'dp')
- out_bias_grad: float32 [2048], P('dp')
The draws below stay inside these ranges and needn't reach their ends.
Inputs may be any that keep to these rules, and one draw needn't show every extreme that they name: `segments`: in each sequence the numbers start at 0 and rise by one at the first token of each document; documents are whole multiples of 128 tokens; some sequence is a single document and some sequence has eight.
All inputs are finite; a program needn't handle non-finite values.
Results may differ from the reference program's by a relative error of at most 0.012.
The reference program's roundings to bfloat16 on the way count: a program that leaves them out, or rounds other values in their place, can miss the bound.
Values may be sent and summed in bfloat16 or wider, within the bound.
A program may use at most 192 MiB of HBM per device.

```python
import math
import jax
import jax.numpy as jnp
from jax import lax

HEADS = 32
HEAD_DIM = 64
ROT = 32
FF = 8192
D = 2048
SEQ_LEN = 1024
SEQS = 16
TOKENS = 16384


def draw_segments(key, part):
    key = jax.random.fold_in(key, 11)
    key_flags, key_single, key_full = jax.random.split(key, 3)
    flags = jax.random.randint(key_flags, (SEQS, 8), 0, 2).astype(jnp.int32)
    column_ids = jnp.arange(8, dtype=jnp.int32)[None, :]
    row_ids = jnp.arange(SEQS, dtype=jnp.int32)[:, None]
    flags = jnp.where(column_ids == 0, 1, flags)
    single_row = jax.random.randint(key_single, (), 0, SEQS).astype(jnp.int32)
    full_row = (single_row + 1 + jax.random.randint(key_full, (), 0, SEQS - 1).astype(jnp.int32)) % SEQS
    flags = jnp.where(row_ids == single_row, jnp.where(column_ids == 0, 1, 0), flags)
    flags = jnp.where(row_ids == full_row, 1, flags)
    block_numbers = jnp.cumsum(flags, axis=1) - 1
    return jnp.repeat(block_numbers, SEQ_LEN // 8, axis=1).astype(jnp.int32)


def draw_cotangent(key, part):
    key = jax.random.fold_in(key, 7)
    key_base = jax.random.fold_in(key, 0)
    row_ids = jnp.arange(TOKENS, dtype=jnp.float32)
    ramp = 1.0 + 2.0 * row_ids / (TOKENS - 1)
    values = jnp.clip(jax.random.normal(key_base, (TOKENS, D), jnp.float32), -4.0, 4.0) * ramp[:, None]
    return values.astype(jnp.bfloat16)


def steps_of(key, dims, shards, least, top_value):
    factor_of = 1.0
    for position, blocks in shards:
        draws = jax.random.uniform(jax.random.fold_in(jax.random.fold_in(key, 6), position), (blocks,), jnp.float32, least / len(shards), top_value / len(shards))
        factor_of = factor_of * jnp.repeat(jnp.exp(draws), dims[position] // blocks).reshape((-1,) + (1,) * (len(dims) - 1 - position))
    return factor_of


def scatter_about(key, shape, scale, limit, cuts=(), kind=jnp.bfloat16):
    gain = steps_of(key, shape, cuts, -0.22, 0.18) if cuts else 1.0
    entries = jax.random.normal(key, shape, jnp.float32) * scale * gain
    return jnp.minimum(jnp.maximum(entries, -limit), limit).astype(kind)


def setup_inputs(seed: int = 0) -> dict:
    streams_of = jax.random.split(jax.random.key(seed), 13)
    return {
        "tokens": scatter_about(streams_of[0], (TOKENS, D), 1.0, 6.0, ((0, 128),)),
        "segments": draw_segments(jax.random.fold_in(streams_of[12], 71), 0),
        "norm_gain": jnp.clip(jnp.exp(math.log(1.59375) - 1.3862944 * jax.random.uniform(streams_of[2], (D,), jnp.float32) ** steps_of(streams_of[2], (D,), ((0, 16),), -0.2, 0.2)), 0.3984375, 1.59375).astype(jnp.bfloat16),
        "norm_shift": scatter_about(streams_of[3], (D,), 0.6, 3.5, ((0, 16),)),
        "qkv_weight": scatter_about(streams_of[4], (D, 3, D), D ** -0.5, 0.125, ((0, 16), (2, 8))),
        "qkv_bias": scatter_about(streams_of[5], (3, HEADS, HEAD_DIM), 0.5, 3.0, ((1, 8), (2, 16))),
        "up_weight": scatter_about(streams_of[6], (D, FF), D ** -0.5, 0.125, ((0, 16), (1, 8))),
        "up_bias": scatter_about(streams_of[7], (FF // HEAD_DIM, HEAD_DIM), 1.0, 6.0, ((0, 8), (1, 16))),
        "out_weight": scatter_about(streams_of[8], (D, D), (max(D // 256, 2)) ** -0.5, 2.0, ((0, 8), (1, 16))),
        "down_weight": scatter_about(streams_of[9], (FF, D), FF ** -0.5, 0.0625, ((0, 8), (1, 16))),
        "out_bias": scatter_about(streams_of[10], (D,), 1.0, 6.0, ((0, 16),)),
        "cotangent": draw_cotangent(jax.random.fold_in(streams_of[12], 71), 0),
    }


highest = lax.Precision.HIGHEST

@jax.custom_vjp
def low(v):
    return lax.optimization_barrier(v.astype(jnp.bfloat16)).astype(jnp.float32)

@jax.custom_vjp
def low_back(v):
    return v

def low_keep(v):
    return (low(v), None)

def low_pass(kept, grad):
    return (grad,)

def back_keep(v):
    return (v, None)

def back_low(kept, grad):
    return (low(grad),)
low.defvjp(low_keep, low_pass)
low_back.defvjp(back_keep, back_low)

def norm_rows(values, gain_row, shift_row):
    centre = values - lax.optimization_barrier(jnp.mean(values, -1, keepdims=True))
    spread = lax.optimization_barrier(jnp.mean(centre * centre, -1, keepdims=True))
    return centre * lax.rsqrt(spread + 1e-05) * gain_row + shift_row

def doc_positions(segment_rows):
    length = segment_rows.shape[-1]
    position_ids = jnp.arange(length, dtype=jnp.int32)
    before = jnp.concatenate([segment_rows[..., :1] - 1, segment_rows[..., :-1]], -1)
    starts = jnp.where(segment_rows != before, position_ids, 0).astype(jnp.int32)
    return position_ids - lax.cummax(starts, axis=segment_rows.ndim - 1)

def rotary_tables(positions):
    half_rot = ROT // 2
    frequency = 10000.0 ** (-jnp.arange(half_rot, dtype=jnp.float32) * 2.0 / ROT)
    angles = positions.astype(jnp.float32)[..., None] * frequency
    return (jnp.cos(angles)[..., None, :], jnp.sin(angles)[..., None, :])

def rotate(values, cosine, sine_table):
    half_rot = ROT // 2
    first_half = values[..., :half_rot]
    second = values[..., half_rot:ROT]
    return jnp.concatenate([first_half * cosine - second * sine_table, second * cosine + first_half * sine_table, values[..., ROT:]], -1)

def attend(queries, key_rows, value_rows, allowed):
    scores = jnp.einsum('bqhe,bkhe->bhqk', queries, key_rows, precision=highest) * HEAD_DIM ** (-0.5)
    scores = low_back(scores)
    scores = jnp.where(allowed[:, None], scores, -1e+30)
    row_max = lax.optimization_barrier(jnp.max(scores, -1, keepdims=True))
    exponent = jnp.exp(scores - row_max)
    weights = exponent / lax.optimization_barrier(jnp.sum(exponent, -1, keepdims=True))
    return jnp.einsum('bhqk,bkhe->bqhe', low(weights), value_rows, precision=highest)

def forward(inputs, params, segment_rows):
    norm_gain, norm_shift, qkv_weight, qkv_bias, up_weight, up_bias, out_weight, down_weight, out_bias = params
    batch_size, length = (inputs.shape[0], inputs.shape[1])
    hidden = low(norm_rows(inputs, norm_gain, norm_shift))
    projected = low_back(jnp.einsum('bld,dce->blce', hidden, qkv_weight, precision=highest) + qkv_bias.reshape(3, D))
    cosine, sine_table = rotary_tables(doc_positions(segment_rows))
    queries = low(rotate(projected[:, :, 0].reshape(batch_size, length, HEADS, HEAD_DIM), cosine, sine_table))
    key_rows = low(rotate(projected[:, :, 1].reshape(batch_size, length, HEADS, HEAD_DIM), cosine, sine_table))
    value_rows = low(projected[:, :, 2].reshape(batch_size, length, HEADS, HEAD_DIM))
    block_rows = min(512, length)
    position_ids = jnp.arange(length, dtype=jnp.int32)
    pieces = []
    for block_start in range(0, length, block_rows):
        query_ids = position_ids[block_start:block_start + block_rows]
        allowed = (position_ids[None, None, :] <= query_ids[None, :, None]) & (segment_rows[:, block_start:block_start + block_rows, None] == segment_rows[:, None, :])
        pieces.append(jax.checkpoint(attend)(queries[:, block_start:block_start + block_rows], key_rows, value_rows, allowed))
    attended = low(low_back(jnp.concatenate(pieces, 1).reshape(batch_size, length, D)))
    up_values = low_back(jnp.einsum('bld,df->blf', hidden, up_weight, precision=highest) + up_bias.reshape(FF))
    activated = low(jax.nn.gelu(up_values, approximate=True))
    attn_part = jnp.einsum('ble,ed->bld', attended, out_weight, precision=highest)
    mlp_part = jnp.einsum('blf,fd->bld', activated, down_weight, precision=highest)
    return inputs + attn_part + mlp_part + out_bias

def reference(tokens, segments, norm_gain, norm_shift, qkv_weight, qkv_bias, up_weight, up_bias, out_weight, down_weight, out_bias, cotangent):
    params = tuple((weight_arg.astype(jnp.float32) for weight_arg in (norm_gain, norm_shift, qkv_weight, qkv_bias, up_weight, up_bias, out_weight, down_weight, out_bias)))
    group_size = 4
    step_count = SEQS // group_size
    input_groups = tokens.reshape(step_count, group_size, SEQ_LEN, D)
    segment_groups = segments.reshape(step_count, group_size, SEQ_LEN)
    cotangent_groups = cotangent.reshape(step_count, group_size, SEQ_LEN, D)

    def advance(running, batch_item):
        inputs_now, segment_now, cotangent_now = batch_item

        def apply_layer(values, *weight_list):
            return forward(values, weight_list, segment_now)
        result, pullback = jax.vjp(apply_layer, inputs_now.astype(jnp.float32), *params)
        gradients = pullback(cotangent_now.astype(jnp.float32))
        running = tuple((total + fresh for total, fresh in zip(running, gradients[1:])))
        return (running, (result.astype(jnp.bfloat16), gradients[0].astype(jnp.bfloat16)))
    zeros_start = tuple((jnp.zeros_like(weight_arg) for weight_arg in params))
    running, (outputs, input_grads) = lax.scan(advance, zeros_start, (input_groups, segment_groups, cotangent_groups))
    return (outputs.reshape(TOKENS, D), input_grads.reshape(TOKENS, D), running[0], running[1], running[2], running[3], running[4], running[5], running[6], running[7], running[8])
```

```python
from types import SimpleNamespace

import jax
import jax.numpy as jnp
from jax import lax
from jax.experimental import pallas as pl
from jax.experimental.pallas import tpu as pltpu
from jax.sharding import PartitionSpec as P

HEAD_DIM = 64
ROT = 32
MESH = pl.DeviceIdType.MESH
BF16 = jnp.bfloat16
F32 = jnp.float32


class Place:
    def __init__(self):
        dp = lax.axis_index("dp")
        mp = lax.axis_index("mp")
        self.dp, self.mp = dp, mp
        self.zl, self.x, self.c = dp // 8, (dp // 2) % 4, dp % 2
        self.y, self.zh = mp // 2, mp % 2
        self.core = (dp + 1 - 2 * self.c, mp)
        self.zlow = (lax.rem(dp + 8, 16), mp)
        self.xp = (self.dp_block(0, 1), mp)
        self.xm = (self.dp_block(0, 3), mp)
        self.yp = (dp, self.mp_block(1, 0))
        self.ym = (dp, self.mp_block(3, 0))
        self.zhigh = (dp, self.mp_block(0, 1))
        self.along_dp = [(lax.rem(dp + d, 16), mp) for d in range(1, 16)]
        self.along_mp = [(dp, lax.rem(mp + d, 8)) for d in range(1, 8)]

    def dp_block(self, dzl, dx, dc=0):
        return ((self.zl + dzl) % 2) * 8 + ((self.x + dx) % 4) * 2 + (self.c + dc) % 2

    def mp_block(self, dy, dzh):
        return ((self.y + dy) % 4) * 2 + (self.zh + dzh) % 2

    def greet(self):
        barrier = pltpu.get_barrier_semaphore()
        partners = self.along_dp + self.along_mp
        for partner in partners:
            pl.semaphore_signal(barrier, inc=1, device_id=partner, device_id_type=MESH)
        pl.semaphore_wait(barrier, len(partners))


class Copies:
    def __init__(self, send_sems):
        self.send_sems = send_sems
        self.count = 0
        self.going = []

    def send(self, src, dst, recv_sem, device, owner=None):
        copy = pltpu.make_async_remote_copy(
            src_ref=src,
            dst_ref=dst,
            send_sem=self.send_sems.at[self.count],
            recv_sem=recv_sem,
            device_id=device,
            device_id_type=MESH,
        )
        copy.start()
        self.count += 1
        self.going.append((owner, copy))

    def finish(self, owners=None):
        for owner, copy in self.going:
            if owners is None or owner in owners:
                copy.wait_send()
        self.going = [] if owners is None else [g for g in self.going if g[0] not in owners]


def arrived(dst, recv_sem, copies, device):
    pltpu.make_async_remote_copy(
        src_ref=dst,
        dst_ref=dst,
        send_sem=copies.send_sems.at[0],
        recv_sem=recv_sem,
        device_id=device,
        device_id_type=MESH,
    ).wait_recv()


ROWS = 256


def rows_at(i, size):
    return pl.ds(i * size if isinstance(i, int) else pl.multiple_of(i * size, size), size)


def nt_dot(a, b):
    return lax.dot_general(a, b, (((1,), (1,)), ((), ())), preferred_element_type=F32)


def nn_dot(a, b):
    return jnp.dot(a, b, preferred_element_type=F32)


def half_of_lanes(values, head):
    lane = lax.broadcasted_iota(jnp.int32, values.shape, 1)
    return jnp.where((lane < HEAD_DIM) == (head == 0), values, jnp.zeros_like(values))


def partner_lanes(values):
    lane = lax.broadcasted_iota(jnp.int32, values.shape, 1)
    on = pltpu.roll(values, values.shape[1] - ROT // 2, 1)
    back = pltpu.roll(values, ROT // 2, 1)
    return jnp.where(lane % HEAD_DIM < ROT // 2, on, back)


def first_rows(segments):
    marks = [segments[0, 128 * b] for b in range(8)]
    return [
        128 * sum((marks[e] < marks[b]).astype(jnp.int32) for e in range(8)) for b in range(8)
    ]


def fill_tables(segments, cosine, sine):
    starts = first_rows(segments)
    step = lax.broadcasted_iota(jnp.int32, (1, 128), 1) % (ROT // 2)
    frequency = jnp.zeros((1, 128), F32)
    for i in range(ROT // 2):
        frequency = jnp.where(step == i, 10000.0 ** (-2.0 * i / ROT), frequency)
    lane = lax.broadcasted_iota(jnp.int32, (128, 128), 1) % HEAD_DIM
    row = lax.broadcasted_iota(jnp.int32, (128, 128), 0)
    for b in range(8):
        position = (row + (128 * b - starts[b])).astype(F32)
        angle = position * frequency
        at = pl.ds(128 * b, 128)
        cosine[at, :] = jnp.where(lane < ROT, jnp.cos(angle), 1.0)
        wave = jnp.sin(angle)
        sine[at, :] = jnp.where(lane < ROT // 2, -wave, jnp.where(lane < ROT, wave, 0.0))


def norm_block(rows_ref, gain, shift, hidden, block):
    step = 32

    def body(i, carry):
        values = rows_ref[block, rows_at(i, step), :].astype(F32)
        centre = values - jnp.mean(values, -1, keepdims=True)
        spread = jnp.mean(centre * centre, -1, keepdims=True)
        normed = centre * lax.rsqrt(spread + 1e-05) * gain[0:1, :] + shift[0:1, :]
        at = pl.ds(pl.multiple_of(block * 128 + i * step, step), step)
        hidden[at, :] = normed.astype(BF16)
        return carry

    lax.fori_loop(0, 128 // step, body, 0)


def transpose_rows(src, dst, i):
    def body(j, carry):
        dst[rows_at(j, ROWS), rows_at(i, ROWS)] = src[rows_at(i, ROWS), rows_at(j, ROWS)].T
        return carry

    lax.fori_loop(0, src.shape[1] // ROWS, body, 0)


def project(i, hidden, weight, bias, cosine, sine, out):
    at = rows_at(i, ROWS)
    for c in range(3):
        values = nn_dot(hidden[at, :], weight[c]) + bias[0:1, c * 256 : c * 256 + 256]
        for slab in range(2):
            part = values[:, slab * 128 : slab * 128 + 128]
            if c < 2:
                part = part * cosine[at, :] + partner_lanes(part) * sine[at, :]
            if c == 0:
                part = part * HEAD_DIM**-0.5
            out[at, c * 256 + slab * 128 : c * 256 + slab * 128 + 128] = part.astype(BF16)


def attend_pair(pair, segments, segment_row, heads, keys_t, values_t, probs, attended_t):
    marks = [segments[0, 128 * b] for b in range(8)]
    key_id = lax.broadcasted_iota(jnp.int32, (ROWS, ROWS), 0)
    query_id = lax.broadcasted_iota(jnp.int32, (ROWS, ROWS), 1)
    later = jnp.where(key_id > query_id, -1e30, 0.0)
    for i in range(1024 // ROWS):
        length = (i + 1) * ROWS
        at = pl.ds(i * ROWS, ROWS)
        queries = heads[at, rows_at(pair, 128)]
        keys = heads[0:length, rows_at(2 + pair, 128)]
        query_segment = segment_row[0:1, i * ROWS : i * ROWS + ROWS]
        for head in range(2):
            scores = nt_dot(keys, half_of_lanes(queries, head))
            pieces = []
            for b in range(2 * (i + 1)):
                piece = scores[b * 128 : b * 128 + 128, :]
                piece = piece + jnp.where(query_segment == marks[b], 0.0, -1e30)
                if b >= 2 * i:
                    piece = piece + later[(b - 2 * i) * 128 : (b - 2 * i) * 128 + 128, :]
                pieces.append(piece)
            scores = jnp.concatenate(pieces, 0)
            exponent = jnp.exp(scores - jnp.max(scores, 0, keepdims=True))
            total = jnp.sum(exponent, 0, keepdims=True)
            weights = (exponent * (1.0 / total)).astype(BF16)
            probs[i][2 * pair + head, :, :] = weights
            at_head = pl.ds(pl.multiple_of(pair * 128 + head * HEAD_DIM, HEAD_DIM), HEAD_DIM)
            attended_t[at_head, at] = nn_dot(values_t[at_head, 0:length], weights).astype(BF16)


def feed_forward(i, hidden, weight, bias, activated, activated_t, slope):
    scale = (2.0 / jnp.pi) ** 0.5
    at = rows_at(i, ROWS)

    def body(j, carry):
        cols = rows_at(j, 512)
        up = nn_dot(hidden[at, :], weight[:, cols]) + bias[0:1, cols]
        square = up * up
        wave = jnp.tanh(scale * up * (1.0 + 0.044715 * square))
        half = 0.5 * (1.0 + wave)
        value = (up * half).astype(BF16)
        activated[at, cols] = value
        activated_t[cols, at] = value.T
        bend = (0.5 * scale) * up * (1.0 - wave * wave) * (1.0 + (3.0 * 0.044715) * square)
        slope[at, cols] = (half + bend).astype(BF16)
        return carry

    lax.fori_loop(0, 2, body, 0)


def partial_output(i, attended, activated, out_weight, down_weight, parts):
    at = rows_at(i, ROWS)

    def body(j, carry):
        cols = rows_at(j, 1024)
        total = nn_dot(attended[at, :], out_weight[:, cols]) + nn_dot(activated[at, :], down_weight[:, cols])
        parts[2 * i, :, cols] = total[:128].astype(BF16)
        parts[2 * i + 1, :, cols] = total[128:].astype(BF16)
        return carry

    lax.fori_loop(0, 2, body, 0)


class TokenGather:
    def __init__(self, place, copies, own, full, sems):
        self.p, self.k, self.own, self.full, self.sems = place, copies, own, full, sems
        half = own.shape[0] // 2
        self.low, self.high = pl.ds(0, half), pl.ds(half, half)

    def block(self, dy, dzh, half=None):
        block = self.full.at[self.p.mp_block(dy, dzh)]
        return block if half is None else block.at[half, :]

    def push(self, src, dy, dzh, slot, device, half=None):
        self.k.send(src, self.block(dy, dzh, half), self.sems.at[slot], device, self)

    def wait(self, dy, dzh, slot, half=None):
        arrived(self.block(dy, dzh, half), self.sems.at[slot], self.k, self.p.yp)

    def step0z(self):
        self.push(self.own, 0, 0, 0, self.p.zhigh)

    def step0y(self):
        self.push(self.own, 0, 0, 1, self.p.yp)
        self.push(self.own, 0, 0, 3, self.p.ym)

    def step1(self):
        self.wait(0, 1, 0)
        self.push(self.block(0, 1), 0, 1, 2, self.p.yp)
        self.push(self.block(0, 1), 0, 1, 4, self.p.ym)

    def step2(self):
        self.wait(3, 0, 1)
        self.push(self.block(3, 0, self.low), 3, 0, 5, self.p.yp, self.low)
        self.wait(1, 0, 3)
        self.push(self.block(1, 0, self.high), 1, 0, 6, self.p.ym, self.high)

    def step3(self):
        self.wait(2, 0, 5, self.low)
        self.wait(2, 0, 6, self.high)
        self.push(self.block(2, 0), 2, 0, 7, self.p.zhigh)

    def step4(self):
        self.wait(3, 1, 2)
        self.wait(1, 1, 4)

    def step5(self):
        self.wait(2, 1, 7)


class Direct:
    def __init__(self, place, copies, devices, block_at, sems):
        self.p, self.k, self.devices, self.block_at, self.sems = place, copies, devices, block_at, sems

    def push(self, src, place_there, i):
        self.k.send(src, place_there, self.sems.at[i], self.devices[i], self)

    def wait(self, i):
        arrived(self.block_at(i), self.sems.at[i], self.k, self.devices[i])

    def wait_all(self):
        for i in range(len(self.devices)):
            self.wait(i)


class WeightGather:
    def __init__(self, place, copies, own, full, sems, block_at):
        self.p, self.k, self.own, self.full, self.sems = place, copies, own, full, sems
        self.block_at = block_at

    def block(self, dzl, dx, dc=0):
        return self.block_at(self.full, self.p.dp_block(dzl, dx, dc))

    def push(self, src, dzl, dx, slot, device):
        self.k.send(src, self.block(dzl, dx), self.sems.at[slot], device, self)

    def wait(self, dzl, dx, slot, dc=0):
        arrived(self.block(dzl, dx, dc), self.sems.at[slot], self.k, self.p.xp)

    def share(self, dzl, dx, slot):
        self.push(self.block(dzl, dx), dzl, dx, 8 + slot, self.p.core)

    def step0(self):
        self.push(self.own, 0, 0, 0, self.p.zlow)
        self.push(self.own, 0, 0, 1, self.p.xp)
        self.push(self.own, 0, 0, 3, self.p.xm)
        self.push(self.own, 0, 0, 7, self.p.core)

    def step1(self):
        self.wait(1, 0, 0)
        self.push(self.block(1, 0), 1, 0, 2, self.p.xp)
        self.push(self.block(1, 0), 1, 0, 4, self.p.xm)
        self.share(1, 0, 0)

    def step2(self):
        self.wait(0, 3, 1)
        self.push(self.block(0, 3), 0, 3, 5, self.p.xp)
        self.share(0, 3, 1)
        self.wait(1, 1, 4)
        self.push(self.block(1, 1), 1, 1, 6, self.p.xm)
        self.share(1, 1, 4)

    def step3(self):
        self.wait(1, 3, 2)
        self.share(1, 3, 2)
        self.wait(0, 1, 3)
        self.share(0, 1, 3)
        self.wait(0, 2, 5)
        self.share(0, 2, 5)
        self.wait(1, 2, 6)
        self.share(1, 2, 6)

    def step4(self):
        self.wait(0, 0, 7, 1)
        self.wait(1, 0, 8, 1)
        self.wait(0, 3, 9, 1)
        self.wait(1, 3, 10, 1)
        self.wait(0, 1, 11, 1)
        self.wait(1, 1, 12, 1)
        self.wait(0, 2, 13, 1)
        self.wait(1, 2, 14, 1)


def block_of_rows(ref, i):
    rows = ref.shape[0] // 16
    return ref.at[pl.ds(pl.multiple_of(i * rows, rows), rows), :]


def block_of_layers(ref, i):
    return ref.at[:, rows_at(i, 128), :]


def block_of_columns(ref, i):
    return ref.at[:, pl.ds(pl.multiple_of(i * 128, 128), 128)]


def spread_bias(bias, dp, dim):
    lane = lax.broadcasted_iota(jnp.int32, (4, HEAD_DIM), 1)
    row = lax.broadcasted_iota(jnp.int32, (4, HEAD_DIM), 0)
    lanes = (lane == 4 * dp + row).astype(BF16)
    return lax.dot_general(
        bias, lanes, (((dim,), (0,)), ((), ())), preferred_element_type=F32
    ).astype(BF16)


class RowBlocks:
    def __init__(self, ref):
        self.ref = ref

    @property
    def at(self):
        return self

    def __getitem__(self, i):
        return self.ref.at[rows_at(i, 128), :]


class ColumnBlocks(RowBlocks):
    def __getitem__(self, i):
        return self.ref.at[:, rows_at(i, 128)]


class LayerBlocks(RowBlocks):
    def __getitem__(self, i):
        return self.ref.at[:, rows_at(i, 128), :]


def add_rows(dst, *terms):
    if len(dst.shape) == 3:
        for c in range(dst.shape[0]):
            add_rows(dst.at[c], *[term.at[c] for term in terms])
        return
    rows = dst.shape[0]
    step = min(rows, 32)

    def body(i, carry):
        at = pl.ds(pl.multiple_of(i * step, step), step)
        total = terms[0][at, :].astype(F32)
        for term in terms[1:]:
            total = total + term[at, :].astype(F32)
        dst[at, :] = total.astype(dst.dtype)
        return carry

    lax.fori_loop(0, rows // step, body, 0)


class TokenReduce:
    def __init__(self, place, copies, part, recv, sems):
        self.p, self.k, self.part, self.recv, self.sems = place, copies, part, recv, sems
        half = recv.shape[1] // 2
        self.low, self.high = pl.ds(0, half), pl.ds(half, half)

    def place_of(self, slot, half=None):
        return self.recv.at[slot] if half is None else self.recv.at[slot, half, :]

    def push(self, src, slot, sem, device, half=None):
        self.k.send(src, self.place_of(slot, half), self.sems.at[sem], device, self)

    def wait(self, slot, sem, half=None):
        arrived(self.place_of(slot, half), self.sems.at[sem], self.k, self.p.yp)

    def send_far(self):
        self.push(self.part(2, 1), 6, 7, self.p.zhigh)

    def send_near(self):
        self.push(self.part(3, 1), 1, 1, self.p.ym)
        self.push(self.part(1, 1), 2, 2, self.p.yp)

    def send_half(self):
        self.push(self.part(3, 0).at[self.high, :], 3, 8, self.p.ym, self.high)
        self.push(self.part(1, 0).at[self.low, :], 4, 9, self.p.yp, self.low)

    def step1(self):
        self.wait(6, 7)
        add_rows(self.recv.at[6], self.recv.at[6], self.part(2, 0))
        self.push(self.place_of(6, self.low), 5, 5, self.p.ym, self.low)
        self.push(self.place_of(6, self.high), 5, 6, self.p.yp, self.high)

    def step2(self):
        low, high = self.place_of(5, self.low), self.place_of(5, self.high)
        self.wait(5, 5, self.low)
        add_rows(low, low, self.part(3, 0).at[self.low, :])
        self.push(low, 3, 3, self.p.ym, self.low)
        self.wait(5, 6, self.high)
        add_rows(high, high, self.part(1, 0).at[self.high, :])
        self.push(high, 4, 4, self.p.yp, self.high)

    def step3(self):
        self.wait(1, 1)
        self.wait(2, 2)
        add_rows(self.recv.at[1], self.recv.at[1], self.recv.at[2], self.part(0, 1))
        self.push(self.recv.at[1], 0, 0, self.p.zhigh)

    def step4(self):
        self.wait(0, 0)
        self.wait(3, 3, self.low)
        self.wait(3, 8, self.high)
        self.wait(4, 9, self.low)
        self.wait(4, 4, self.high)
        return (self.recv.at[0], self.recv.at[3], self.recv.at[4], self.part(0, 0))


class WeightReduce:
    def __init__(self, place, copies, recv, sems, result):
        self.p, self.k, self.recv, self.sems = place, copies, recv, sems
        self.result = result

    def push(self, src, slot, device):
        self.k.send(src, self.recv.at[slot], self.sems.at[slot], device, self)

    def wait(self, slot):
        arrived(self.recv.at[slot], self.sems.at[slot], self.k, self.p.xp)

    def give(self, src, dzl, dx):
        self.push(src, 7 + 4 * dzl + dx, self.p.core)

    def pair(self, dzl, dx):
        return self.recv.at[7 + 4 * dzl + dx]

    def take(self, dzl, dx):
        self.wait(7 + 4 * dzl + dx)
        return self.pair(dzl, dx)

    def pass_on(self, dx):
        if dx == 2:
            self.push(self.pair(0, 2), 5, self.p.xm)
            self.push(self.pair(1, 2), 6, self.p.xp)
        if dx == 3:
            self.push(self.pair(1, 3), 1, self.p.xm)
        if dx == 1:
            self.push(self.pair(0, 1), 2, self.p.xp)

    def step2(self):
        self.wait(5)
        add_rows(self.recv.at[5], self.recv.at[5], self.pair(0, 3))
        self.push(self.recv.at[5], 3, self.p.xm)
        self.wait(6)
        add_rows(self.recv.at[6], self.recv.at[6], self.pair(1, 1))
        self.push(self.recv.at[6], 4, self.p.xp)

    def step3(self):
        self.wait(1)
        self.wait(4)
        add_rows(self.recv.at[1], self.recv.at[1], self.recv.at[4], self.pair(1, 0))
        self.push(self.recv.at[1], 0, self.p.zlow)

    def step4(self):
        self.wait(2)
        self.wait(3)
        self.wait(0)
        add_rows(self.result, self.recv.at[0], self.recv.at[2], self.recv.at[3], self.pair(0, 0))


ORDER = (2, 3, 1, 0)


def small_reduce(side, parts):
    for dx in ORDER:
        for dzl in range(2):
            side.give(parts.at[side.p.dp_block(dzl, dx, 1)], dzl, dx)
    for dx in ORDER:
        for dzl in range(2):
            pair = side.take(dzl, dx)
            pair[...] = pair[...] + parts[side.p.dp_block(dzl, dx)]
        side.pass_on(dx)


def column_share(side, left, right, stage_at, dx, core):
    blocks = [side.p.dp_block(dzl, dx, core) for dzl in range(2)]
    taken = [None if core else side.take(dzl, dx) for dzl in range(2)]
    wide = jnp.concatenate([right[:, rows_at(b, 128)] for b in blocks], 1)
    step = min(left.shape[0], 512)

    def body(i, carry):
        at = rows_at(i, step)
        product = nn_dot(left[at, :], wide)
        for dzl in range(2):
            half = product[:, dzl * 128 : dzl * 128 + 128]
            if core:
                stage_at(4 * dzl + dx)[at, :] = half.astype(BF16)
            else:
                taken[dzl][at, :] = (half + taken[dzl][at, :].astype(F32)).astype(BF16)
        return carry

    lax.fori_loop(0, left.shape[0] // step, body, 0)
    if core:
        for dzl in range(2):
            side.give(stage_at(4 * dzl + dx), dzl, dx)
    else:
        side.pass_on(dx)


def row_share(side, left, right, piece, stage_at, dx, core):
    blocks = [side.p.dp_block(dzl, dx, core) for dzl in range(2)]
    taken = [None if core else side.take(dzl, dx) for dzl in range(2)]
    tall = jnp.concatenate([left[rows_at(b, 128), :] for b in blocks], 0)
    step = 256

    for j in range(right.shape[1] // step):
        product = nn_dot(tall, right[:, j * step : j * step + step])
        for dzl in range(2):
            half = product[dzl * 128 : dzl * 128 + 128]
            if core:
                piece(stage_at(4 * dzl + dx), j)[...] = half.astype(BF16)
            else:
                place = piece(taken[dzl], j)
                place[...] = (half + place[...].astype(F32)).astype(BF16)
    if core:
        for dzl in range(2):
            side.give(stage_at(4 * dzl + dx), dzl, dx)
    else:
        side.pass_on(dx)


def columns_of(block, j):
    return block.at[:, j * 256 : j * 256 + 256]


def layer_of(block, j):
    return block.at[j]


def back_gelu(i, cotangent, down, out, slope, grad_attended):
    at = rows_at(i, ROWS)
    rows = cotangent[at, :]
    slope[at, :] = (nt_dot(rows, down[...]) * slope[at, :].astype(F32)).astype(BF16)
    grad_attended[at, :] = nt_dot(rows, out[...]).astype(BF16)


def back_hidden(i, grads, grad_up, qkv, up, parts):
    at = rows_at(i, ROWS)

    def body(j, carry):
        cols = rows_at(j, 1024)
        total = nt_dot(grad_up[at, :], up[cols, :])
        for c in range(3):
            total = total + nt_dot(grads[at, c * 256 : c * 256 + 256], qkv[c, cols, :])
        parts[at, cols] = total.astype(BF16)
        return carry

    lax.fori_loop(0, 2, body, 0)


def attend_back(pair, heads, keys_t, probs, grad_attended, cosine, sine, keys_sum, values_sum, turned, grads):
    keys_sum[...] = jnp.zeros_like(keys_sum)
    values_sum[...] = jnp.zeros_like(values_sum)
    here = rows_at(pair, 128)
    for i in range(1024 // ROWS):
        length = (i + 1) * ROWS
        at = pl.ds(i * ROWS, ROWS)
        queries = heads[at, here]
        values = heads[0:length, rows_at(4 + pair, 128)]
        grad_rows = grad_attended[at, here]
        for head in range(2):
            weights = probs[i][2 * pair + head]
            grad_own = half_of_lanes(grad_rows, head)
            grad_weights = nt_dot(values, grad_own)
            wide = weights.astype(F32)
            inner = jnp.sum(wide * grad_weights, 0, keepdims=True)
            grad_scores = (wide * (grad_weights - inner)).astype(BF16)
            keys_sum[0:length, :] += nn_dot(grad_scores, half_of_lanes(queries, head))
            values_sum[0:length, :] += nn_dot(weights, grad_own)
            at_head = pl.ds(pl.multiple_of(pair * 128 + head * HEAD_DIM, HEAD_DIM), HEAD_DIM)
            turned[head * HEAD_DIM : head * HEAD_DIM + HEAD_DIM, :] = nn_dot(
                keys_t[at_head, 0:length], grad_scores
            )
        grad_queries = turned[...].T * HEAD_DIM**-0.5
        grads[at, here] = (
            grad_queries * cosine[at, :] - partner_lanes(grad_queries) * sine[at, :]
        ).astype(BF16)

    def finish(i, carry):
        at = rows_at(i, 128)
        grad_keys = keys_sum[at, :]
        grads[at, rows_at(2 + pair, 128)] = (
            grad_keys * cosine[at, :] - partner_lanes(grad_keys) * sine[at, :]
        ).astype(BF16)
        grads[at, rows_at(4 + pair, 128)] = values_sum[at, :].astype(BF16)
        return carry

    lax.fori_loop(0, 8, finish, 0)


def column_sums(ref, total):
    def body(i, carry):
        return carry + jnp.sum(ref[rows_at(i, 64), :].astype(F32), 0, keepdims=True)

    zero = jnp.zeros((1, ref.shape[1]), F32)
    total[0:1, 0 : ref.shape[1]] = lax.fori_loop(0, ref.shape[0] // 64, body, zero)


def finish_outputs(terms, tokens, vectors, outputs):
    def body(i, carry):
        at = rows_at(i, 32)
        total = sum(term[at, :].astype(F32) for term in terms)
        total = total + tokens[at, :].astype(F32) + vectors[2:3, :]
        outputs[at, :] = total.astype(BF16)
        return carry

    lax.fori_loop(0, 4, body, 0)


def finish_norm(terms, tokens, cotangent, vectors, input_grad, sums):
    sums[...] = jnp.zeros_like(sums)

    def body(i, carry):
        at = rows_at(i, 16)
        grad = sum(term[at, :].astype(F32) for term in terms)
        values = tokens[at, :].astype(F32)
        centre = values - jnp.mean(values, -1, keepdims=True)
        scale = lax.rsqrt(jnp.mean(centre * centre, -1, keepdims=True) + 1e-05)
        normed = centre * scale
        sums[0:1, :] += jnp.sum(grad * normed, 0, keepdims=True)
        sums[1:2, :] += jnp.sum(grad, 0, keepdims=True)
        grad = grad * vectors[0:1, :]
        back = grad - jnp.mean(grad, -1, keepdims=True)
        back = (back - normed * jnp.mean(grad * normed, -1, keepdims=True)) * scale
        input_grad[at, :] = (cotangent[at, :].astype(F32) + back).astype(BF16)
        return carry

    lax.fori_loop(0, 8, body, 0)


WEIGHTS = dict(qkv=(3, 128, 256), up=(128, 1024), out=(256, 128), down=(1024, 128))
SMALL = dict(bias=(32, 128), norm=(8, 128))

SCRATCH = dict(
    seq_rows=((8, 128, 2048), BF16),
    cot_rows=((1024, 2048), BF16),
    hidden=((1024, 2048), BF16),
    hidden_t=((2048, 1024), BF16),
    qkv_full=((3, 2048, 256), BF16),
    up_full=((2048, 1024), BF16),
    out_full=((256, 2048), BF16),
    down_full=((1024, 2048), BF16),
    heads=((1024, 768), BF16),
    keys_t=((256, 1024), BF16),
    values_t=((256, 1024), BF16),
    probs0=((4, 256, 256), BF16),
    probs1=((4, 512, 256), BF16),
    probs2=((4, 768, 256), BF16),
    probs3=((4, 1024, 256), BF16),
    attended=((1024, 256), BF16),
    attended_t=((256, 1024), BF16),
    activated=((1024, 1024), BF16),
    activated_t=((1024, 1024), BF16),
    slope=((1024, 1024), BF16),
    cosine=((1024, 128), F32),
    sine=((1024, 128), F32),
    vectors=((8, 2048), F32),
    keys_sum=((1024, 128), F32),
    values_sum=((1024, 128), F32),
    turned=((128, 256), F32),
    bias_own=((48, 128), BF16),
    bias_full=((16, 48, 128), BF16),
    qkv_bias=((8, 768), F32),
    up_bias=((8, 1024), F32),
    first_recv=((7, 128, 2048), BF16),
    second_recv=((7, 128, 2048), BF16),
    bias_recv=((15, 32, 128), F32),
    norm_recv=((15, 8, 128), F32),
    bias_parts=((16, 32, 128), F32),
    norm_parts=((16, 8, 128), F32),
    bias_row=((8, 2048), F32),
    norm_sums=((8, 2048), F32),
    norm_own=((8, 128), F32),
    norm_full=((7, 8, 128), F32),
    tokens_here=((128, 2048), BF16),
    cotangent_here=((128, 2048), BF16),
    gain_here=((1, 128), BF16),
    shift_here=((1, 128), BF16),
    out_bias_here=((1, 128), BF16),
    qkv_bias_here=((3, 4, 4), BF16),
    up_bias_here=((4, 16), BF16),
    segment_row=((1, 1024), jnp.int32),
)
RESULTS = dict(
    outputs=((128, 2048), BF16),
    input_grad=((128, 2048), BF16),
    **{name: (shape, F32) for name, shape in WEIGHTS.items()},
    **{name: (shape, F32) for name, shape in SMALL.items()},
)


def layer_kernel(*refs):
    tokens, cotangent, qkv_own, up_own, out_own, down_own = refs[:6]
    vectors_own, segments_own = refs[6:11], refs[11]
    results_out = refs[12 : 12 + len(RESULTS)]
    refs = refs[12 + len(RESULTS) :]
    here = SimpleNamespace(**dict(zip(SCRATCH, refs)))
    refs = refs[len(SCRATCH) :]
    results = refs[: len(RESULTS)]
    outputs, input_grad, *sums, norm_grad = results
    segments = refs[len(RESULTS)]
    send_sems, token_sems, weight_sems, sum_sems, part_sems, direct_sems, local_sems, free_sems = refs[
        len(RESULTS) + 1 :
    ]
    vectors, hidden, cot_rows = here.vectors, here.hidden, here.cot_rows
    activated, slope = here.activated, here.slope
    bias_own, bias_full = here.bias_own, here.bias_full
    bias_parts, bias_row = here.bias_parts, here.bias_row
    probs = [here.probs0, here.probs1, here.probs2, here.probs3]
    grad_attended = activated.at[:, 0:256]
    grads = activated.at[:, 256:1024]
    place = Place()
    copies = Copies(send_sems)

    leaving = []

    def leave(*which):
        for i in which:
            copy = pltpu.make_async_copy(results[i], results_out[i], local_sems.at[15 + i])
            copy.start()
            leaving.append(copy)

    def row_block(dy):
        return (place.y + dy) % 4

    loads = [
        pltpu.make_async_copy(src, dst, local_sems.at[i])
        for i, (src, dst) in enumerate(
            [
                *zip(
                    vectors_own,
                    (
                        here.gain_here,
                        here.shift_here,
                        here.out_bias_here,
                        here.qkv_bias_here,
                        here.up_bias_here,
                    ),
                ),
                (segments_own, segments),
                (segments_own, here.segment_row),
                (tokens, here.tokens_here),
                (cotangent, here.cotangent_here),
            ]
        )
    ]
    for load in loads:
        load.start()
    for load in loads[:5]:
        load.wait()

    bias_own[...] = jnp.zeros_like(bias_own)
    bias_own[0:1, :] = here.gain_here[...]
    bias_own[1:2, :] = here.shift_here[...]
    bias_own[2:3, :] = here.out_bias_here[...]
    for c in range(3):
        bias_own[16 + 4 * c : 20 + 4 * c, 0:HEAD_DIM] = spread_bias(here.qkv_bias_here[c], place.dp, 1)
    bias_own[32:48, 0:HEAD_DIM] = spread_bias(here.up_bias_here[...], place.dp, 0)

    place.greet()
    seq = TokenGather(place, copies, tokens, here.seq_rows, token_sems.at[0])
    cot = TokenGather(place, copies, cotangent, RowBlocks(cot_rows), token_sems.at[1])
    qkv, up, out, down = [
        WeightGather(place, copies, own, full, weight_sems.at[i], block_at)
        for i, (own, full, block_at) in enumerate(
            (
                (qkv_own, here.qkv_full, block_of_layers),
                (up_own, here.up_full, block_of_rows),
                (out_own, here.out_full, block_of_columns),
                (down_own, here.down_full, block_of_columns),
            )
        )
    ]
    bias = Direct(
        place,
        copies,
        place.along_dp,
        lambda i: bias_full.at[lax.rem(place.dp + 15 - i, 16)],
        direct_sems.at[0],
    )
    for i in range(15):
        bias.push(bias_own, bias_full.at[place.dp], i)
    seq.step0z()
    seq.step0y()
    qkv.step0()
    bias_full[pl.ds(place.dp, 1)] = bias_own[...][None]
    own_copies = []
    for i, each in enumerate((seq, cot, qkv, up, out, down)):
        own_copies.append(pltpu.make_async_copy(each.own, each.block(0, 0), local_sems.at[9 + i]))
        own_copies[-1].start()
    for load in loads[5:]:
        load.wait()
    fill_tables(segments, here.cosine, here.sine)
    bias.wait_all()
    for i in range(16):
        at = slice(128 * i, 128 * i + 128)
        vectors[0:3, at] = bias_full[i, 0:3, :].astype(F32)
    summed = jnp.sum(bias_full[:, 16:48, 0:HEAD_DIM].astype(F32), 0)
    for r in range(12):
        here.qkv_bias[0:1, r * HEAD_DIM : r * HEAD_DIM + HEAD_DIM] = summed[r : r + 1]
    for r in range(16):
        here.up_bias[0:1, r * HEAD_DIM : r * HEAD_DIM + HEAD_DIM] = summed[16 + r : 17 + r]

    def norm_rows(dy, dzh):
        norm_block(
            here.seq_rows, vectors.at[0:1], vectors.at[1:2], hidden, place.mp_block(dy, dzh)
        )

    def turn_rows(dy):
        transpose_rows(hidden, here.hidden_t, row_block(dy))

    def project_rows(dy):
        project(
            row_block(dy),
            hidden,
            here.qkv_full,
            here.qkv_bias,
            here.cosine,
            here.sine,
            here.heads,
        )

    def feed_rows(dy):
        feed_forward(
            row_block(dy), hidden, here.up_full, here.up_bias, activated, here.activated_t, slope
        )

    def attend(pair):
        attend_pair(
            pair,
            segments,
            here.segment_row,
            here.heads,
            here.keys_t,
            here.values_t,
            probs,
            here.attended_t,
        )

    own_copies[0].wait()
    norm_rows(0, 0)
    qkv.step1()
    up.step0()
    seq.step2()
    seq.step1()
    norm_rows(3, 0)
    norm_rows(1, 0)
    qkv.step2()
    norm_rows(0, 1)
    turn_rows(0)
    up.step1()
    down.step0()
    out.step0()
    seq.step3()
    cot.step0z()
    qkv.step3()
    norm_rows(2, 0)
    qkv.step4()
    own_copies[2].wait()
    project_rows(0)
    up.step2()
    seq.step4()
    cot.step0y()
    norm_rows(3, 1)
    norm_rows(1, 1)
    project_rows(3)
    project_rows(1)
    seq.step5()
    up.step3()
    norm_rows(2, 1)
    project_rows(2)
    for slab in range(2):
        at = slice(slab * 128, slab * 128 + 128)
        here.keys_t[at, :] = here.heads[:, 256 + slab * 128 : 384 + slab * 128].T
        here.values_t[at, :] = here.heads[:, 512 + slab * 128 : 640 + slab * 128].T
    down.step1()
    out.step1()
    up.step4()
    cot.step2()
    cot.step1()
    attend(0)
    down.step2()
    out.step2()
    cot.step3()
    attend(1)
    down.step3()
    out.step3()
    for i in range(2):
        at = slice(i * 128, i * 128 + 128)
        here.attended[:, at] = here.attended_t[at, :].T
    own_copies[3].wait()
    feed_rows(0)
    feed_rows(1)
    feed_rows(2)
    feed_rows(3)
    down.step4()
    out.step4()
    own_copies[4].wait()
    own_copies[5].wait()
    copies.finish([seq])

    hidden_blocks = RowBlocks(hidden)
    first = TokenReduce(
        place,
        copies,
        lambda dy, dzh: here.seq_rows.at[place.mp_block(dy, dzh)],
        here.first_recv,
        part_sems.at[0],
    )
    second = TokenReduce(
        place,
        copies,
        lambda dy, dzh: hidden_blocks[place.mp_block(dy, dzh)],
        here.second_recv,
        part_sems.at[1],
    )
    recv = (
        LayerBlocks(here.qkv_full),
        RowBlocks(here.up_full),
        ColumnBlocks(here.out_full),
        ColumnBlocks(here.down_full),
        here.bias_recv,
    )
    qkv_sum, up_sum, out_sum, down_sum, bias_sum = [
        WeightReduce(place, copies, recv[i], sum_sems.at[i], sums[i])
        for i in range(5)
    ]

    def output_rows(dy):
        partial_output(
            row_block(dy),
            here.attended,
            activated,
            here.out_full,
            here.down_full,
            here.seq_rows,
        )

    for dy in ORDER:
        output_rows(dy)

    def back_rows(dy):
        back_gelu(row_block(dy), cot_rows, here.down_full, here.out_full, slope, grad_attended)

    own_copies[1].wait()
    cot.step4()
    cot.step5()
    first.send_far()
    first.send_near()
    for dy in range(4):
        back_rows(dy)

    def release(which, *sides):
        copies.finish(sides)
        for device in (place.core, place.xp, place.xm, place.zlow):
            pl.semaphore_signal(free_sems.at[which], inc=1, device_id=device, device_id_type=MESH)

    def claim(which):
        pl.semaphore_wait(free_sems.at[which], 4)

    release(0, out, down)
    copies.finish([cot])
    for dy in range(1, 4):
        turn_rows(dy)
    column_sums(cot_rows, bias_row)
    bias_parts[...] = jnp.zeros_like(bias_parts)
    for i in range(16):
        bias_parts[i, 0:1, :] = bias_row[0:1, 128 * i : 128 * i + 128]
    claim(0)

    def stage_down(i):
        return hidden.at[:, i * 128 : i * 128 + 128]

    def stage_out(i):
        return hidden.at[0:256, 1024 + i * 128 : 1152 + i * 128]

    for dx in ORDER:
        column_share(down_sum, here.activated_t, cot_rows, stage_down, dx, 1)
    for dx in ORDER:
        column_share(out_sum, here.attended_t, cot_rows, stage_out, dx, 1)
    for dx in ORDER:
        column_share(down_sum, here.activated_t, cot_rows, stage_down, dx, 0)
    first.step1()
    first.send_half()
    for dx in ORDER:
        column_share(out_sum, here.attended_t, cot_rows, stage_out, dx, 0)

    def attend_rows(pair):
        attend_back(
            pair,
            here.heads,
            here.keys_t,
            probs,
            grad_attended,
            here.cosine,
            here.sine,
            here.keys_sum,
            here.values_sum,
            here.turned,
            grads,
        )

    attend_rows(0)
    first.step2()
    down_sum.step2()
    out_sum.step2()
    attend_rows(1)
    copies.finish([down_sum, out_sum])

    def hidden_rows(dy):
        back_hidden(row_block(dy), grads, slope, here.qkv_full, here.up_full, hidden)

    hidden_rows(2)
    second.send_far()
    hidden_rows(3)
    hidden_rows(1)
    second.send_near()
    hidden_rows(0)
    release(1, qkv, up)
    first.step3()
    down_sum.step3()
    out_sum.step3()
    column_sums(slope, bias_row)
    for r in range(16):
        piece = bias_row[0:1, r * HEAD_DIM : r * HEAD_DIM + HEAD_DIM]
        bias_parts[0, 16 + r : 17 + r, 0:HEAD_DIM] = piece
    column_sums(grads, bias_row)
    for r in range(12):
        piece = bias_row[0:1, r * HEAD_DIM : r * HEAD_DIM + HEAD_DIM]
        bias_parts[0, 4 + r : 5 + r, 0:HEAD_DIM] = piece
    for i in range(1, 16):
        bias_parts[i, 4:32, :] = bias_parts[0, 4:32, :]

    def stage_up(i):
        return cot_rows.at[i * 128 : i * 128 + 128, 0:1024]

    def stage_qkv(i):
        return here.probs3.at[pl.ds(0, 3), i * 128 : i * 128 + 128, :]

    second.step1()
    second.send_half()
    claim(1)
    for dx in ORDER:
        row_share(up_sum, here.hidden_t, slope, columns_of, stage_up, dx, 1)
    second.step2()
    for dx in ORDER:
        row_share(qkv_sum, here.hidden_t, grads, layer_of, stage_qkv, dx, 1)
    for dx in ORDER:
        row_share(up_sum, here.hidden_t, slope, columns_of, stage_up, dx, 0)
    second.step3()
    for dx in ORDER:
        row_share(qkv_sum, here.hidden_t, grads, layer_of, stage_qkv, dx, 0)
    small_reduce(bias_sum, bias_parts)
    finish_outputs(first.step4(), here.tokens_here, vectors, outputs)
    leave(0)
    up_sum.step2()
    down_sum.step4()
    out_sum.step4()
    leave(4, 5)
    qkv_sum.step2()
    bias_sum.step2()
    finish_norm(
        second.step4(), here.tokens_here, here.cotangent_here, vectors, input_grad, here.norm_sums
    )
    leave(1)
    for i in range(16):
        here.norm_parts[i, :, :] = here.norm_sums[:, 128 * i : 128 * i + 128]
    norm_recv, norm_own, norm_full = here.norm_recv, here.norm_own, here.norm_full
    norm_sum = Direct(place, copies, place.along_dp, lambda i: norm_recv.at[i], direct_sems.at[1])
    for i in range(15):
        norm_sum.push(here.norm_parts.at[lax.rem(place.dp + i + 1, 16)], norm_recv.at[i], i)
    up_sum.step3()
    qkv_sum.step3()
    bias_sum.step3()
    norm_sum.wait_all()
    norm_own[...] = jnp.sum(norm_recv[...], 0) + here.norm_parts[place.dp]
    norm_all = Direct(place, copies, place.along_mp, lambda i: norm_full.at[i], direct_sems.at[2])
    for i in range(7):
        norm_all.push(norm_own, norm_full.at[i], i)
    up_sum.step4()
    qkv_sum.step4()
    bias_sum.step4()
    leave(2, 3, 6)
    norm_all.wait_all()
    total = norm_own[...] + jnp.sum(norm_full[...], 0)
    norm_grad[...] = pltpu.roll(total, (128 - 16 * place.mp) % 128, 1)
    leave(7)
    copies.finish()
    for copy in leaving:
        copy.wait()


def layer(tokens, cotangent, weights, vectors, segments):
    anywhere = pl.BlockSpec(memory_space=pl.ANY)
    return pl.pallas_call(
        layer_kernel,
        out_shape=[jax.ShapeDtypeStruct(*spec) for spec in RESULTS.values()],
        in_specs=[anywhere] * 12,
        out_specs=[anywhere] * len(RESULTS),
        scratch_shapes=[pltpu.VMEM(*spec) for spec in (*SCRATCH.values(), *RESULTS.values())]
        + [
            pltpu.SMEM((1, 1024), jnp.int32),
            pltpu.SemaphoreType.DMA((2 * 8 + 4 * 15 + 2 * 10 + 5 * 15 + 37,)),
            pltpu.SemaphoreType.DMA((2, 8)),
            pltpu.SemaphoreType.DMA((4, 15)),
            pltpu.SemaphoreType.DMA((5, 15)),
            pltpu.SemaphoreType.DMA((2, 10)),
            pltpu.SemaphoreType.DMA((3, 15)),
            pltpu.SemaphoreType.DMA((23,)),
            pltpu.SemaphoreType.REGULAR((2,)),
        ],
        compiler_params=pltpu.CompilerParams(
            collective_id=1, has_side_effects=True, vmem_limit_bytes=63 * 2**20
        ),
        name="layer",
    )(tokens, cotangent, *weights, *vectors, segments)


def hand_over_kernel(*refs):
    large, small, large_out = refs[:6], refs[6:8], refs[8:14]
    qkv_bias, up_bias, out_bias, gain, shift, sems = refs[14:]
    moves = [
        pltpu.make_async_copy(src, dst, sems.at[i]) for i, (src, dst) in enumerate(zip(large, large_out))
    ]
    for move in moves:
        move.start()
    bias, norm = small
    dp = lax.axis_index("dp")
    out_bias[...] = bias[0:1, :]
    gain[...] = norm[0:1, 0:16]
    shift[...] = norm[1:2, 0:16]
    mine = pltpu.roll(bias[...], (128 - 4 * dp) % 128, 1)
    for c in range(3):
        qkv_bias[c] = mine[4 + 4 * c : 8 + 4 * c, 0:4]
    up_bias[...] = mine[16:32, :].T[0:4, :]
    for move in moves:
        move.wait()


def hand_over(results):
    anywhere = pl.BlockSpec(memory_space=pl.ANY)
    vmem = pl.BlockSpec(memory_space=pltpu.VMEM)
    small = [(3, 4, 4), (4, 16), (1, 128), (1, 16), (1, 16)]
    return pl.pallas_call(
        hand_over_kernel,
        out_shape=[jax.ShapeDtypeStruct(r.shape, r.dtype) for r in results[:6]]
        + [jax.ShapeDtypeStruct(shape, F32) for shape in small],
        in_specs=[vmem] * 8,
        out_specs=[anywhere] * 6 + [vmem] * 5,
        scratch_shapes=[pltpu.SemaphoreType.DMA((6,))],
        name="hand_over",
    )(*results)


def on_device(
    tokens,
    segments,
    norm_gain,
    norm_shift,
    qkv_weight,
    qkv_bias,
    up_weight,
    up_bias,
    out_weight,
    down_weight,
    out_bias,
    cotangent,
):
    results = layer(
        tokens,
        cotangent,
        (qkv_weight.transpose(1, 0, 2), up_weight, out_weight, down_weight),
        (norm_gain[None], norm_shift[None], out_bias[None], qkv_bias, up_bias.T),
        segments,
    )
    outputs, input_grad, qkv, up, out, down, qkv_b, up_b, out_b, gain, shift = hand_over(results)
    return (
        outputs,
        input_grad,
        gain[0],
        shift[0],
        qkv.transpose(1, 0, 2),
        qkv_b,
        up,
        up_b.T,
        out,
        down,
        out_b[0],
    )


def solution(mesh):
    return jax.shard_map(
        on_device,
        mesh=mesh,
        in_specs=(
            P(("dp", "mp"), None),
            P("dp", None),
            P("dp"),
            P("dp"),
            P("dp", None, "mp"),
            P(None, "mp", "dp"),
            P("dp", "mp"),
            P("mp", "dp"),
            P("mp", "dp"),
            P("mp", "dp"),
            P("dp"),
            P(("dp", "mp"), None),
        ),
        out_specs=(
            P(("dp", "mp"), None),
            P(("dp", "mp"), None),
            P(("dp", "mp")),
            P(("dp", "mp")),
            P("dp", None, "mp"),
            P(None, "mp", "dp"),
            P("dp", "mp"),
            P("mp", "dp"),
            P("mp", "dp"),
            P("mp", "dp"),
            P("dp"),
        ),
        check_vma=False,
    )
```

```python
from types import SimpleNamespace

import jax
import jax.numpy as jnp
from jax import lax
from jax.experimental import pallas as pl
from jax.experimental.pallas import tpu as pltpu
from jax.sharding import PartitionSpec as P

HEAD_DIM = 64
ROT = 32
MESH = pl.DeviceIdType.MESH
BF16 = jnp.bfloat16
F32 = jnp.float32


class Place:
    def __init__(self):
        dp = lax.axis_index("dp")
        mp = lax.axis_index("mp")
        self.dp, self.mp = dp, mp
        self.zl, self.x, self.c = dp // 8, (dp // 2) % 4, dp % 2
        self.y, self.zh = mp // 2, mp % 2
        self.core = (dp + 1 - 2 * self.c, mp)
        self.zlow = (lax.rem(dp + 8, 16), mp)
        self.xp = (self.dp_block(0, 1), mp)
        self.xm = (self.dp_block(0, 3), mp)
        self.yp = (dp, self.mp_block(1, 0))
        self.ym = (dp, self.mp_block(3, 0))
        self.zhigh = (dp, self.mp_block(0, 1))
        self.along_dp = [(lax.rem(dp + d, 16), mp) for d in range(1, 16)]
        self.along_mp = [(dp, lax.rem(mp + d, 8)) for d in range(1, 8)]

    def dp_block(self, dzl, dx, dc=0):
        return ((self.zl + dzl) % 2) * 8 + ((self.x + dx) % 4) * 2 + (self.c + dc) % 2

    def mp_block(self, dy, dzh):
        return ((self.y + dy) % 4) * 2 + (self.zh + dzh) % 2

    def greet(self):
        barrier = pltpu.get_barrier_semaphore()
        partners = self.along_dp + self.along_mp
        for partner in partners:
            pl.semaphore_signal(barrier, inc=1, device_id=partner, device_id_type=MESH)
        pl.semaphore_wait(barrier, len(partners))


class Copies:
    def __init__(self, send_sems):
        self.send_sems = send_sems
        self.count = 0
        self.going = []

    def send(self, src, dst, recv_sem, device, owner=None):
        copy = pltpu.make_async_remote_copy(
            src_ref=src,
            dst_ref=dst,
            send_sem=self.send_sems.at[self.count],
            recv_sem=recv_sem,
            device_id=device,
            device_id_type=MESH,
        )
        copy.start()
        self.count += 1
        self.going.append((owner, copy))

    def finish(self, owners=None):
        for owner, copy in self.going:
            if owners is None or owner in owners:
                copy.wait_send()
        self.going = [] if owners is None else [g for g in self.going if g[0] not in owners]


def arrived(dst, recv_sem, copies, device):
    pltpu.make_async_remote_copy(
        src_ref=dst,
        dst_ref=dst,
        send_sem=copies.send_sems.at[0],
        recv_sem=recv_sem,
        device_id=device,
        device_id_type=MESH,
    ).wait_recv()


ROWS = 256


def rows_at(i, size):
    return pl.ds(i * size if isinstance(i, int) else pl.multiple_of(i * size, size), size)


def nt_dot(a, b):
    return lax.dot_general(a, b, (((1,), (1,)), ((), ())), preferred_element_type=F32)


def nn_dot(a, b):
    return jnp.dot(a, b, preferred_element_type=F32)


def half_of_lanes(values, head):
    lane = lax.broadcasted_iota(jnp.int32, values.shape, 1)
    return jnp.where((lane < HEAD_DIM) == (head == 0), values, jnp.zeros_like(values))


def partner_lanes(values):
    lane = lax.broadcasted_iota(jnp.int32, values.shape, 1)
    on = pltpu.roll(values, values.shape[1] - ROT // 2, 1)
    back = pltpu.roll(values, ROT // 2, 1)
    return jnp.where(lane % HEAD_DIM < ROT // 2, on, back)


def first_rows(segments):
    marks = [segments[0, 128 * b] for b in range(8)]
    return [
        128 * sum((marks[e] < marks[b]).astype(jnp.int32) for e in range(8)) for b in range(8)
    ]


def fill_tables(segments, cosine, sine):
    starts = first_rows(segments)
    step = lax.broadcasted_iota(jnp.int32, (1, 128), 1) % (ROT // 2)
    frequency = jnp.zeros((1, 128), F32)
    for i in range(ROT // 2):
        frequency = jnp.where(step == i, 10000.0 ** (-2.0 * i / ROT), frequency)
    lane = lax.broadcasted_iota(jnp.int32, (128, 128), 1) % HEAD_DIM
    row = lax.broadcasted_iota(jnp.int32, (128, 128), 0)
    for b in range(8):
        position = (row + (128 * b - starts[b])).astype(F32)
        angle = position * frequency
        at = pl.ds(128 * b, 128)
        cosine[at, :] = jnp.where(lane < ROT, jnp.cos(angle), 1.0)
        wave = jnp.sin(angle)
        sine[at, :] = jnp.where(lane < ROT // 2, -wave, jnp.where(lane < ROT, wave, 0.0))


def norm_block(rows_ref, gain, shift, hidden, block):
    step = 32

    def body(i, carry):
        values = rows_ref[block, rows_at(i, step), :].astype(F32)
        centre = values - jnp.mean(values, -1, keepdims=True)
        spread = jnp.mean(centre * centre, -1, keepdims=True)
        normed = centre * lax.rsqrt(spread + 1e-05) * gain[0:1, :] + shift[0:1, :]
        at = pl.ds(pl.multiple_of(block * 128 + i * step, step), step)
        hidden[at, :] = normed.astype(BF16)
        return carry

    lax.fori_loop(0, 128 // step, body, 0)


def transpose_rows(src, dst, i):
    def body(j, carry):
        dst[rows_at(j, ROWS), rows_at(i, ROWS)] = src[rows_at(i, ROWS), rows_at(j, ROWS)].T
        return carry

    lax.fori_loop(0, src.shape[1] // ROWS, body, 0)


def project(i, hidden, weight, bias, cosine, sine, out):
    at = rows_at(i, ROWS)
    for c in range(3):
        values = nn_dot(hidden[at, :], weight[c]) + bias[0:1, c * 256 : c * 256 + 256]
        for slab in range(2):
            part = values[:, slab * 128 : slab * 128 + 128]
            if c < 2:
                part = part * cosine[at, :] + partner_lanes(part) * sine[at, :]
            if c == 0:
                part = part * HEAD_DIM**-0.5
            out[at, c * 256 + slab * 128 : c * 256 + slab * 128 + 128] = part.astype(BF16)


def attend_pair(pair, segments, segment_row, heads, keys_t, values_t, probs, attended_t):
    marks = [segments[0, 128 * b] for b in range(8)]
    key_id = lax.broadcasted_iota(jnp.int32, (ROWS, ROWS), 0)
    query_id = lax.broadcasted_iota(jnp.int32, (ROWS, ROWS), 1)
    later = jnp.where(key_id > query_id, -1e30, 0.0)
    for i in range(1024 // ROWS):
        length = (i + 1) * ROWS
        at = pl.ds(i * ROWS, ROWS)
        queries = heads[at, rows_at(pair, 128)]
        keys = heads[0:length, rows_at(2 + pair, 128)]
        query_segment = segment_row[0:1, i * ROWS : i * ROWS + ROWS]
        for head in range(2):
            scores = nt_dot(keys, half_of_lanes(queries, head))
            pieces = []
            for b in range(2 * (i + 1)):
                piece = scores[b * 128 : b * 128 + 128, :]
                piece = piece + jnp.where(query_segment == marks[b], 0.0, -1e30)
                if b >= 2 * i:
                    piece = piece + later[(b - 2 * i) * 128 : (b - 2 * i) * 128 + 128, :]
                pieces.append(piece)
            scores = jnp.concatenate(pieces, 0)
            exponent = jnp.exp(scores - jnp.max(scores, 0, keepdims=True))
            total = jnp.sum(exponent, 0, keepdims=True)
            weights = (exponent * (1.0 / total)).astype(BF16)
            probs[i][2 * pair + head, :, :] = weights
            at_head = pl.ds(pl.multiple_of(pair * 128 + head * HEAD_DIM, HEAD_DIM), HEAD_DIM)
            attended_t[at_head, at] = nn_dot(values_t[at_head, 0:length], weights).astype(BF16)


def feed_forward(i, hidden, weight, bias, activated, activated_t, slope):
    scale = (2.0 / jnp.pi) ** 0.5
    at = rows_at(i, ROWS)

    def body(j, carry):
        cols = rows_at(j, 512)
        up = nn_dot(hidden[at, :], weight[:, cols]) + bias[0:1, cols]
        square = up * up
        wave = jnp.tanh(scale * up * (1.0 + 0.044715 * square))
        half = 0.5 * (1.0 + wave)
        value = (up * half).astype(BF16)
        activated[at, cols] = value
        activated_t[cols, at] = value.T
        bend = (0.5 * scale) * up * (1.0 - wave * wave) * (1.0 + (3.0 * 0.044715) * square)
        slope[at, cols] = (half + bend).astype(BF16)
        return carry

    lax.fori_loop(0, 2, body, 0)


def partial_output(i, attended, activated, out_weight, down_weight, parts):
    at = rows_at(i, ROWS)

    def body(j, carry):
        cols = rows_at(j, 1024)
        total = nn_dot(attended[at, :], out_weight[:, cols]) + nn_dot(activated[at, :], down_weight[:, cols])
        parts[2 * i, :, cols] = total[:128].astype(BF16)
        parts[2 * i + 1, :, cols] = total[128:].astype(BF16)
        return carry

    lax.fori_loop(0, 2, body, 0)


class TokenGather:
    def __init__(self, place, copies, own, full, sems):
        self.p, self.k, self.own, self.full, self.sems = place, copies, own, full, sems
        half = own.shape[0] // 2
        self.low, self.high = pl.ds(0, half), pl.ds(half, half)

    def block(self, dy, dzh, half=None):
        block = self.full.at[self.p.mp_block(dy, dzh)]
        return block if half is None else block.at[half, :]

    def push(self, src, dy, dzh, slot, device, half=None):
        self.k.send(src, self.block(dy, dzh, half), self.sems.at[slot], device, self)

    def wait(self, dy, dzh, slot, half=None):
        arrived(self.block(dy, dzh, half), self.sems.at[slot], self.k, self.p.yp)

    def step0z(self):
        self.push(self.own, 0, 0, 0, self.p.zhigh)

    def step0y(self):
        self.push(self.own, 0, 0, 1, self.p.yp)
        self.push(self.own, 0, 0, 3, self.p.ym)

    def step1(self):
        self.wait(0, 1, 0)
        self.push(self.block(0, 1), 0, 1, 2, self.p.yp)
        self.push(self.block(0, 1), 0, 1, 4, self.p.ym)

    def step2(self):
        self.wait(3, 0, 1)
        self.push(self.block(3, 0, self.low), 3, 0, 5, self.p.yp, self.low)
        self.wait(1, 0, 3)
        self.push(self.block(1, 0, self.high), 1, 0, 6, self.p.ym, self.high)

    def step3(self):
        self.wait(2, 0, 5, self.low)
        self.wait(2, 0, 6, self.high)
        self.push(self.block(2, 0), 2, 0, 7, self.p.zhigh)

    def step4(self):
        self.wait(3, 1, 2)
        self.wait(1, 1, 4)

    def step5(self):
        self.wait(2, 1, 7)


class Direct:
    def __init__(self, place, copies, devices, block_at, sems):
        self.p, self.k, self.devices, self.block_at, self.sems = place, copies, devices, block_at, sems

    def push(self, src, place_there, i):
        self.k.send(src, place_there, self.sems.at[i], self.devices[i], self)

    def wait(self, i):
        arrived(self.block_at(i), self.sems.at[i], self.k, self.devices[i])

    def wait_all(self):
        for i in range(len(self.devices)):
            self.wait(i)


class WeightGather:
    def __init__(self, place, copies, own, full, sems, block_at):
        self.p, self.k, self.own, self.full, self.sems = place, copies, own, full, sems
        self.block_at = block_at

    def block(self, dzl, dx, dc=0):
        return self.block_at(self.full, self.p.dp_block(dzl, dx, dc))

    def push(self, src, dzl, dx, slot, device):
        self.k.send(src, self.block(dzl, dx), self.sems.at[slot], device, self)

    def wait(self, dzl, dx, slot, dc=0):
        arrived(self.block(dzl, dx, dc), self.sems.at[slot], self.k, self.p.xp)

    def share(self, dzl, dx, slot):
        self.push(self.block(dzl, dx), dzl, dx, 8 + slot, self.p.core)

    def step0(self):
        self.push(self.own, 0, 0, 0, self.p.zlow)
        self.push(self.own, 0, 0, 1, self.p.xp)
        self.push(self.own, 0, 0, 3, self.p.xm)
        self.push(self.own, 0, 0, 7, self.p.core)

    def step1(self):
        self.wait(1, 0, 0)
        self.push(self.block(1, 0), 1, 0, 2, self.p.xp)
        self.push(self.block(1, 0), 1, 0, 4, self.p.xm)
        self.share(1, 0, 0)

    def step2(self):
        self.wait(0, 3, 1)
        self.push(self.block(0, 3), 0, 3, 5, self.p.xp)
        self.share(0, 3, 1)
        self.wait(1, 1, 4)
        self.push(self.block(1, 1), 1, 1, 6, self.p.xm)
        self.share(1, 1, 4)

    def step3(self):
        self.wait(1, 3, 2)
        self.share(1, 3, 2)
        self.wait(0, 1, 3)
        self.share(0, 1, 3)
        self.wait(0, 2, 5)
        self.share(0, 2, 5)
        self.wait(1, 2, 6)
        self.share(1, 2, 6)

    def step4(self):
        self.wait(0, 0, 7, 1)
        self.wait(1, 0, 8, 1)
        self.wait(0, 3, 9, 1)
        self.wait(1, 3, 10, 1)
        self.wait(0, 1, 11, 1)
        self.wait(1, 1, 12, 1)
        self.wait(0, 2, 13, 1)
        self.wait(1, 2, 14, 1)


def block_of_rows(ref, i):
    rows = ref.shape[0] // 16
    return ref.at[pl.ds(pl.multiple_of(i * rows, rows), rows), :]


def block_of_layers(ref, i):
    return ref.at[:, rows_at(i, 128), :]


def block_of_columns(ref, i):
    return ref.at[:, pl.ds(pl.multiple_of(i * 128, 128), 128)]


def spread_bias(bias, dp, dim):
    lane = lax.broadcasted_iota(jnp.int32, (4, HEAD_DIM), 1)
    row = lax.broadcasted_iota(jnp.int32, (4, HEAD_DIM), 0)
    lanes = (lane == 4 * dp + row).astype(BF16)
    return lax.dot_general(
        bias, lanes, (((dim,), (0,)), ((), ())), preferred_element_type=F32
    ).astype(BF16)


class RowBlocks:
    def __init__(self, ref):
        self.ref = ref

    @property
    def at(self):
        return self

    def __getitem__(self, i):
        return self.ref.at[rows_at(i, 128), :]


class ColumnBlocks(RowBlocks):
    def __getitem__(self, i):
        return self.ref.at[:, rows_at(i, 128)]


class LayerBlocks(RowBlocks):
    def __getitem__(self, i):
        return self.ref.at[:, rows_at(i, 128), :]


def add_rows(dst, *terms):
    if len(dst.shape) == 3:
        for c in range(dst.shape[0]):
            add_rows(dst.at[c], *[term.at[c] for term in terms])
        return
    rows = dst.shape[0]
    step = min(rows, max(16, 32768 // dst.shape[1]))

    def body(i, carry):
        at = pl.ds(pl.multiple_of(i * step, step), step)
        total = terms[0][at, :].astype(F32)
        for term in terms[1:]:
            total = total + term[at, :].astype(F32)
        dst[at, :] = total.astype(dst.dtype)
        return carry

    lax.fori_loop(0, rows // step, body, 0)


class TokenReduce:
    def __init__(self, place, copies, part, recv, sems):
        self.p, self.k, self.part, self.recv, self.sems = place, copies, part, recv, sems
        half = recv.shape[1] // 2
        self.low, self.high = pl.ds(0, half), pl.ds(half, half)

    def place_of(self, slot, half=None):
        return self.recv.at[slot] if half is None else self.recv.at[slot, half, :]

    def push(self, src, slot, sem, device, half=None):
        self.k.send(src, self.place_of(slot, half), self.sems.at[sem], device, self)

    def wait(self, slot, sem, half=None):
        arrived(self.place_of(slot, half), self.sems.at[sem], self.k, self.p.yp)

    def send_far(self):
        self.push(self.part(2, 1), 6, 7, self.p.zhigh)

    def send_near(self):
        self.push(self.part(3, 1), 1, 1, self.p.ym)
        self.push(self.part(1, 1), 2, 2, self.p.yp)

    def send_half(self):
        self.push(self.part(3, 0).at[self.high, :], 3, 8, self.p.ym, self.high)
        self.push(self.part(1, 0).at[self.low, :], 4, 9, self.p.yp, self.low)

    def step1(self):
        self.wait(6, 7)
        add_rows(self.recv.at[6], self.recv.at[6], self.part(2, 0))
        self.push(self.place_of(6, self.low), 5, 5, self.p.ym, self.low)
        self.push(self.place_of(6, self.high), 5, 6, self.p.yp, self.high)

    def step2(self):
        low, high = self.place_of(5, self.low), self.place_of(5, self.high)
        self.wait(5, 5, self.low)
        add_rows(low, low, self.part(3, 0).at[self.low, :])
        self.push(low, 3, 3, self.p.ym, self.low)
        self.wait(5, 6, self.high)
        add_rows(high, high, self.part(1, 0).at[self.high, :])
        self.push(high, 4, 4, self.p.yp, self.high)

    def step3(self):
        self.wait(1, 1)
        self.wait(2, 2)
        add_rows(self.recv.at[1], self.recv.at[1], self.recv.at[2], self.part(0, 1))
        self.push(self.recv.at[1], 0, 0, self.p.zhigh)

    def step4(self):
        self.wait(0, 0)
        self.wait(3, 3, self.low)
        self.wait(3, 8, self.high)
        self.wait(4, 9, self.low)
        self.wait(4, 4, self.high)
        return (self.recv.at[0], self.recv.at[3], self.recv.at[4], self.part(0, 0))


class WeightReduce:
    def __init__(self, place, copies, recv, sems, result):
        self.p, self.k, self.recv, self.sems = place, copies, recv, sems
        self.result = result

    def push(self, src, slot, device):
        self.k.send(src, self.recv.at[slot], self.sems.at[slot], device, self)

    def wait(self, slot):
        arrived(self.recv.at[slot], self.sems.at[slot], self.k, self.p.xp)

    def give(self, src, dzl, dx):
        self.push(src, 7 + 4 * dzl + dx, self.p.core)

    def pair(self, dzl, dx):
        return self.recv.at[7 + 4 * dzl + dx]

    def take(self, dzl, dx):
        self.wait(7 + 4 * dzl + dx)
        return self.pair(dzl, dx)

    def pass_on(self, dx):
        if dx == 2:
            self.push(self.pair(0, 2), 5, self.p.xm)
            self.push(self.pair(1, 2), 6, self.p.xp)
        if dx == 3:
            self.push(self.pair(1, 3), 1, self.p.xm)
        if dx == 1:
            self.push(self.pair(0, 1), 2, self.p.xp)

    def step2(self):
        self.wait(5)
        add_rows(self.recv.at[5], self.recv.at[5], self.pair(0, 3))
        self.push(self.recv.at[5], 3, self.p.xm)
        self.wait(6)
        add_rows(self.recv.at[6], self.recv.at[6], self.pair(1, 1))
        self.push(self.recv.at[6], 4, self.p.xp)

    def step3(self):
        self.wait(1)
        self.wait(4)
        add_rows(self.recv.at[1], self.recv.at[1], self.recv.at[4], self.pair(1, 0))
        self.push(self.recv.at[1], 0, self.p.zlow)

    def step4(self):
        self.wait(2)
        self.wait(3)
        self.wait(0)
        add_rows(self.result, self.recv.at[0], self.recv.at[2], self.recv.at[3], self.pair(0, 0))


ORDER = (2, 3, 1, 0)


def small_reduce(side, parts):
    for dx in ORDER:
        for dzl in range(2):
            side.give(parts.at[side.p.dp_block(dzl, dx, 1)], dzl, dx)
    for dx in ORDER:
        for dzl in range(2):
            pair = side.take(dzl, dx)
            pair[...] = pair[...] + parts[side.p.dp_block(dzl, dx)]
        side.pass_on(dx)


def column_share(side, left, right, stage_at, dx, core):
    blocks = [side.p.dp_block(dzl, dx, core) for dzl in range(2)]
    taken = [None if core else side.take(dzl, dx) for dzl in range(2)]
    wide = jnp.concatenate([right[:, rows_at(b, 128)] for b in blocks], 1)
    step = min(left.shape[0], 512)

    def body(i, carry):
        at = rows_at(i, step)
        product = nn_dot(left[at, :], wide)
        for dzl in range(2):
            half = product[:, dzl * 128 : dzl * 128 + 128]
            if core:
                stage_at(4 * dzl + dx)[at, :] = half.astype(BF16)
            else:
                taken[dzl][at, :] = (half + taken[dzl][at, :].astype(F32)).astype(BF16)
        return carry

    lax.fori_loop(0, left.shape[0] // step, body, 0)
    if core:
        for dzl in range(2):
            side.give(stage_at(4 * dzl + dx), dzl, dx)
    else:
        side.pass_on(dx)


def row_share(side, left, right, piece, stage_at, dx, core):
    blocks = [side.p.dp_block(dzl, dx, core) for dzl in range(2)]
    taken = [None if core else side.take(dzl, dx) for dzl in range(2)]
    tall = jnp.concatenate([left[rows_at(b, 128), :] for b in blocks], 0)
    step = 256

    for j in range(right.shape[1] // step):
        product = nn_dot(tall, right[:, j * step : j * step + step])
        for dzl in range(2):
            half = product[dzl * 128 : dzl * 128 + 128]
            if core:
                piece(stage_at(4 * dzl + dx), j)[...] = half.astype(BF16)
            else:
                place = piece(taken[dzl], j)
                place[...] = (half + place[...].astype(F32)).astype(BF16)
    if core:
        for dzl in range(2):
            side.give(stage_at(4 * dzl + dx), dzl, dx)
    else:
        side.pass_on(dx)


def columns_of(block, j):
    return block.at[:, j * 256 : j * 256 + 256]


def layer_of(block, j):
    return block.at[j]


def back_gelu(i, cotangent, down, out, slope, grad_attended):
    at = rows_at(i, ROWS)
    rows = cotangent[at, :]
    slope[at, :] = (nt_dot(rows, down[...]) * slope[at, :].astype(F32)).astype(BF16)
    grad_attended[at, :] = nt_dot(rows, out[...]).astype(BF16)


def back_hidden(i, grads, grad_up, qkv, up, parts):
    at = rows_at(i, ROWS)

    def body(j, carry):
        cols = rows_at(j, 1024)
        total = nt_dot(grad_up[at, :], up[cols, :])
        for c in range(3):
            total = total + nt_dot(grads[at, c * 256 : c * 256 + 256], qkv[c, cols, :])
        parts[at, cols] = total.astype(BF16)
        return carry

    lax.fori_loop(0, 2, body, 0)


def attend_back(pair, heads, keys_t, probs, grad_attended, cosine, sine, keys_sum, values_sum, turned, grads):
    keys_sum[...] = jnp.zeros_like(keys_sum)
    values_sum[...] = jnp.zeros_like(values_sum)
    here = rows_at(pair, 128)
    for i in range(1024 // ROWS):
        length = (i + 1) * ROWS
        at = pl.ds(i * ROWS, ROWS)
        queries = heads[at, here]
        values = heads[0:length, rows_at(4 + pair, 128)]
        grad_rows = grad_attended[at, here]
        for head in range(2):
            weights = probs[i][2 * pair + head]
            grad_own = half_of_lanes(grad_rows, head)
            grad_weights = nt_dot(values, grad_own)
            wide = weights.astype(F32)
            inner = jnp.sum(wide * grad_weights, 0, keepdims=True)
            grad_scores = (wide * (grad_weights - inner)).astype(BF16)
            keys_sum[0:length, :] += nn_dot(grad_scores, half_of_lanes(queries, head))
            values_sum[0:length, :] += nn_dot(weights, grad_own)
            at_head = pl.ds(pl.multiple_of(pair * 128 + head * HEAD_DIM, HEAD_DIM), HEAD_DIM)
            turned[head * HEAD_DIM : head * HEAD_DIM + HEAD_DIM, :] = nn_dot(
                keys_t[at_head, 0:length], grad_scores
            )
        grad_queries = turned[...].T * HEAD_DIM**-0.5
        grads[at, here] = (
            grad_queries * cosine[at, :] - partner_lanes(grad_queries) * sine[at, :]
        ).astype(BF16)

    def finish(i, carry):
        at = rows_at(i, 128)
        grad_keys = keys_sum[at, :]
        grads[at, rows_at(2 + pair, 128)] = (
            grad_keys * cosine[at, :] - partner_lanes(grad_keys) * sine[at, :]
        ).astype(BF16)
        grads[at, rows_at(4 + pair, 128)] = values_sum[at, :].astype(BF16)
        return carry

    lax.fori_loop(0, 8, finish, 0)


def column_sums(ref, total):
    def body(i, carry):
        return carry + jnp.sum(ref[rows_at(i, 64), :].astype(F32), 0, keepdims=True)

    zero = jnp.zeros((1, ref.shape[1]), F32)
    total[0:1, 0 : ref.shape[1]] = lax.fori_loop(0, ref.shape[0] // 64, body, zero)


def finish_outputs(terms, tokens, vectors, outputs):
    def body(i, carry):
        at = rows_at(i, 32)
        total = sum(term[at, :].astype(F32) for term in terms)
        total = total + tokens[at, :].astype(F32) + vectors[2:3, :]
        outputs[at, :] = total.astype(BF16)
        return carry

    lax.fori_loop(0, 4, body, 0)


def finish_norm(terms, tokens, cotangent, vectors, input_grad, sums):
    sums[...] = jnp.zeros_like(sums)

    def body(i, carry):
        at = rows_at(i, 16)
        grad = sum(term[at, :].astype(F32) for term in terms)
        values = tokens[at, :].astype(F32)
        centre = values - jnp.mean(values, -1, keepdims=True)
        scale = lax.rsqrt(jnp.mean(centre * centre, -1, keepdims=True) + 1e-05)
        normed = centre * scale
        sums[0:1, :] += jnp.sum(grad * normed, 0, keepdims=True)
        sums[1:2, :] += jnp.sum(grad, 0, keepdims=True)
        grad = grad * vectors[0:1, :]
        back = grad - jnp.mean(grad, -1, keepdims=True)
        back = (back - normed * jnp.mean(grad * normed, -1, keepdims=True)) * scale
        input_grad[at, :] = (cotangent[at, :].astype(F32) + back).astype(BF16)
        return carry

    lax.fori_loop(0, 8, body, 0)


WEIGHTS = dict(qkv=(3, 128, 256), up=(128, 1024), out=(256, 128), down=(1024, 128))
SMALL = dict(bias=(32, 128), norm=(8, 128))

SCRATCH = dict(
    seq_rows=((8, 128, 2048), BF16),
    cot_rows=((1024, 2048), BF16),
    hidden=((1024, 2048), BF16),
    hidden_t=((2048, 1024), BF16),
    qkv_full=((3, 2048, 256), BF16),
    up_full=((2048, 1024), BF16),
    out_full=((256, 2048), BF16),
    down_full=((1024, 2048), BF16),
    heads=((1024, 768), BF16),
    keys_t=((256, 1024), BF16),
    values_t=((256, 1024), BF16),
    probs0=((4, 256, 256), BF16),
    probs1=((4, 512, 256), BF16),
    probs2=((4, 768, 256), BF16),
    probs3=((4, 1024, 256), BF16),
    attended=((1024, 256), BF16),
    attended_t=((256, 1024), BF16),
    activated=((1024, 1024), BF16),
    activated_t=((1024, 1024), BF16),
    slope=((1024, 1024), BF16),
    cosine=((1024, 128), F32),
    sine=((1024, 128), F32),
    vectors=((8, 2048), F32),
    keys_sum=((1024, 128), F32),
    values_sum=((1024, 128), F32),
    turned=((128, 256), F32),
    bias_own=((48, 128), BF16),
    bias_full=((16, 48, 128), BF16),
    qkv_bias=((8, 768), F32),
    up_bias=((8, 1024), F32),
    first_recv=((7, 128, 2048), BF16),
    second_recv=((7, 128, 2048), BF16),
    bias_recv=((15, 32, 128), F32),
    norm_recv=((15, 8, 128), F32),
    bias_parts=((16, 32, 128), F32),
    norm_parts=((16, 8, 128), F32),
    bias_row=((8, 2048), F32),
    norm_sums=((8, 2048), F32),
    norm_own=((8, 128), F32),
    norm_full=((7, 8, 128), F32),
    tokens_here=((128, 2048), BF16),
    cotangent_here=((128, 2048), BF16),
    gain_here=((1, 128), BF16),
    shift_here=((1, 128), BF16),
    out_bias_here=((1, 128), BF16),
    qkv_bias_here=((3, 4, 4), BF16),
    up_bias_here=((4, 16), BF16),
    segment_row=((1, 1024), jnp.int32),
)
RESULTS = dict(
    outputs=((128, 2048), BF16),
    input_grad=((128, 2048), BF16),
    **{name: (shape, F32) for name, shape in WEIGHTS.items()},
    **{name: (shape, F32) for name, shape in SMALL.items()},
)


def layer_kernel(*refs):
    tokens, cotangent, qkv_own, up_own, out_own, down_own = refs[:6]
    vectors_own, segments_own = refs[6:11], refs[11]
    results_out = refs[12 : 12 + len(RESULTS)]
    refs = refs[12 + len(RESULTS) :]
    here = SimpleNamespace(**dict(zip(SCRATCH, refs)))
    refs = refs[len(SCRATCH) :]
    results = refs[: len(RESULTS)]
    outputs, input_grad, *sums, norm_grad = results
    segments = refs[len(RESULTS)]
    send_sems, token_sems, weight_sems, sum_sems, part_sems, direct_sems, local_sems, free_sems = refs[
        len(RESULTS) + 1 :
    ]
    vectors, hidden, cot_rows = here.vectors, here.hidden, here.cot_rows
    activated, slope = here.activated, here.slope
    bias_own, bias_full = here.bias_own, here.bias_full
    bias_parts, bias_row = here.bias_parts, here.bias_row
    probs = [here.probs0, here.probs1, here.probs2, here.probs3]
    grad_attended = activated.at[:, 0:256]
    grads = activated.at[:, 256:1024]
    place = Place()
    copies = Copies(send_sems)

    leaving = []

    def leave(*which):
        for i in which:
            copy = pltpu.make_async_copy(results[i], results_out[i], local_sems.at[15 + i])
            copy.start()
            leaving.append(copy)

    def row_block(dy):
        return (place.y + dy) % 4

    loads = [
        pltpu.make_async_copy(src, dst, local_sems.at[i])
        for i, (src, dst) in enumerate(
            [
                *zip(
                    vectors_own,
                    (
                        here.gain_here,
                        here.shift_here,
                        here.out_bias_here,
                        here.qkv_bias_here,
                        here.up_bias_here,
                    ),
                ),
                (segments_own, segments),
                (segments_own, here.segment_row),
                (tokens, here.tokens_here),
                (cotangent, here.cotangent_here),
            ]
        )
    ]
    for load in loads:
        load.start()
    for load in loads[:5]:
        load.wait()

    bias_own[...] = jnp.zeros_like(bias_own)
    bias_own[0:1, :] = here.gain_here[...]
    bias_own[1:2, :] = here.shift_here[...]
    bias_own[2:3, :] = here.out_bias_here[...]
    for c in range(3):
        bias_own[16 + 4 * c : 20 + 4 * c, 0:HEAD_DIM] = spread_bias(here.qkv_bias_here[c], place.dp, 1)
    bias_own[32:48, 0:HEAD_DIM] = spread_bias(here.up_bias_here[...], place.dp, 0)

    place.greet()
    seq = TokenGather(place, copies, tokens, here.seq_rows, token_sems.at[0])
    cot = TokenGather(place, copies, cotangent, RowBlocks(cot_rows), token_sems.at[1])
    qkv, up, out, down = [
        WeightGather(place, copies, own, full, weight_sems.at[i], block_at)
        for i, (own, full, block_at) in enumerate(
            (
                (qkv_own, here.qkv_full, block_of_layers),
                (up_own, here.up_full, block_of_rows),
                (out_own, here.out_full, block_of_columns),
                (down_own, here.down_full, block_of_columns),
            )
        )
    ]
    bias = Direct(
        place,
        copies,
        place.along_dp,
        lambda i: bias_full.at[lax.rem(place.dp + 15 - i, 16)],
        direct_sems.at[0],
    )
    for i in range(15):
        bias.push(bias_own, bias_full.at[place.dp], i)
    seq.step0z()
    seq.step0y()
    qkv.step0()
    bias_full[pl.ds(place.dp, 1)] = bias_own[...][None]
    own_copies = []
    for i, each in enumerate((seq, cot, qkv, up, out, down)):
        own_copies.append(pltpu.make_async_copy(each.own, each.block(0, 0), local_sems.at[9 + i]))
        own_copies[-1].start()
    for load in loads[5:]:
        load.wait()
    fill_tables(segments, here.cosine, here.sine)
    bias.wait_all()
    for i in range(16):
        at = slice(128 * i, 128 * i + 128)
        vectors[0:3, at] = bias_full[i, 0:3, :].astype(F32)
    summed = jnp.sum(bias_full[:, 16:48, 0:HEAD_DIM].astype(F32), 0)
    for r in range(12):
        here.qkv_bias[0:1, r * HEAD_DIM : r * HEAD_DIM + HEAD_DIM] = summed[r : r + 1]
    for r in range(16):
        here.up_bias[0:1, r * HEAD_DIM : r * HEAD_DIM + HEAD_DIM] = summed[16 + r : 17 + r]

    def norm_rows(dy, dzh):
        norm_block(
            here.seq_rows, vectors.at[0:1], vectors.at[1:2], hidden, place.mp_block(dy, dzh)
        )

    def turn_rows(dy):
        transpose_rows(hidden, here.hidden_t, row_block(dy))

    def project_rows(dy):
        project(
            row_block(dy),
            hidden,
            here.qkv_full,
            here.qkv_bias,
            here.cosine,
            here.sine,
            here.heads,
        )

    def feed_rows(dy):
        feed_forward(
            row_block(dy), hidden, here.up_full, here.up_bias, activated, here.activated_t, slope
        )

    def attend(pair):
        attend_pair(
            pair,
            segments,
            here.segment_row,
            here.heads,
            here.keys_t,
            here.values_t,
            probs,
            here.attended_t,
        )

    own_copies[0].wait()
    norm_rows(0, 0)
    qkv.step1()
    up.step0()
    seq.step2()
    seq.step1()
    norm_rows(3, 0)
    norm_rows(1, 0)
    qkv.step2()
    norm_rows(0, 1)
    turn_rows(0)
    up.step1()
    down.step0()
    out.step0()
    seq.step3()
    cot.step0z()
    qkv.step3()
    norm_rows(2, 0)
    qkv.step4()
    own_copies[2].wait()
    project_rows(0)
    up.step2()
    seq.step4()
    cot.step0y()
    norm_rows(3, 1)
    norm_rows(1, 1)
    project_rows(3)
    project_rows(1)
    seq.step5()
    up.step3()
    norm_rows(2, 1)
    project_rows(2)
    for slab in range(2):
        at = slice(slab * 128, slab * 128 + 128)
        here.keys_t[at, :] = here.heads[:, 256 + slab * 128 : 384 + slab * 128].T
        here.values_t[at, :] = here.heads[:, 512 + slab * 128 : 640 + slab * 128].T
    down.step1()
    out.step1()
    up.step4()
    cot.step2()
    cot.step1()
    attend(0)
    down.step2()
    out.step2()
    cot.step3()
    attend(1)
    down.step3()
    out.step3()
    for i in range(2):
        at = slice(i * 128, i * 128 + 128)
        here.attended[:, at] = here.attended_t[at, :].T
    own_copies[3].wait()
    feed_rows(0)
    feed_rows(1)
    feed_rows(2)
    feed_rows(3)
    down.step4()
    out.step4()
    own_copies[4].wait()
    own_copies[5].wait()
    copies.finish([seq])

    hidden_blocks = RowBlocks(hidden)
    first = TokenReduce(
        place,
        copies,
        lambda dy, dzh: here.seq_rows.at[place.mp_block(dy, dzh)],
        here.first_recv,
        part_sems.at[0],
    )
    second = TokenReduce(
        place,
        copies,
        lambda dy, dzh: hidden_blocks[place.mp_block(dy, dzh)],
        here.second_recv,
        part_sems.at[1],
    )
    recv = (
        LayerBlocks(here.qkv_full),
        RowBlocks(here.up_full),
        ColumnBlocks(here.out_full),
        ColumnBlocks(here.down_full),
        here.bias_recv,
    )
    qkv_sum, up_sum, out_sum, down_sum, bias_sum = [
        WeightReduce(place, copies, recv[i], sum_sems.at[i], sums[i])
        for i in range(5)
    ]

    def output_rows(dy):
        partial_output(
            row_block(dy),
            here.attended,
            activated,
            here.out_full,
            here.down_full,
            here.seq_rows,
        )

    for dy in ORDER:
        output_rows(dy)

    def back_rows(dy):
        back_gelu(row_block(dy), cot_rows, here.down_full, here.out_full, slope, grad_attended)

    own_copies[1].wait()
    cot.step4()
    cot.step5()
    first.send_far()
    first.send_near()
    for dy in range(4):
        back_rows(dy)

    def release(which, *sides):
        copies.finish(sides)
        for device in (place.core, place.xp, place.xm, place.zlow):
            pl.semaphore_signal(free_sems.at[which], inc=1, device_id=device, device_id_type=MESH)

    def claim(which):
        pl.semaphore_wait(free_sems.at[which], 4)

    release(0, out, down)
    copies.finish([cot])
    for dy in range(1, 4):
        turn_rows(dy)
    column_sums(cot_rows, bias_row)
    bias_parts[...] = jnp.zeros_like(bias_parts)
    for i in range(16):
        bias_parts[i, 0:1, :] = bias_row[0:1, 128 * i : 128 * i + 128]
    claim(0)

    def stage_down(i):
        return hidden.at[:, i * 128 : i * 128 + 128]

    def stage_out(i):
        return hidden.at[0:256, 1024 + i * 128 : 1152 + i * 128]

    for dx in ORDER:
        column_share(down_sum, here.activated_t, cot_rows, stage_down, dx, 1)
    for dx in ORDER:
        column_share(out_sum, here.attended_t, cot_rows, stage_out, dx, 1)
    for dx in ORDER:
        column_share(down_sum, here.activated_t, cot_rows, stage_down, dx, 0)
    first.step1()
    first.send_half()
    for dx in ORDER:
        column_share(out_sum, here.attended_t, cot_rows, stage_out, dx, 0)

    def attend_rows(pair):
        attend_back(
            pair,
            here.heads,
            here.keys_t,
            probs,
            grad_attended,
            here.cosine,
            here.sine,
            here.keys_sum,
            here.values_sum,
            here.turned,
            grads,
        )

    attend_rows(0)
    first.step2()
    down_sum.step2()
    out_sum.step2()
    attend_rows(1)
    copies.finish([down_sum, out_sum])

    def hidden_rows(dy):
        back_hidden(row_block(dy), grads, slope, here.qkv_full, here.up_full, hidden)

    hidden_rows(2)
    second.send_far()
    hidden_rows(3)
    hidden_rows(1)
    second.send_near()
    hidden_rows(0)
    release(1, qkv, up)
    first.step3()
    down_sum.step3()
    out_sum.step3()
    column_sums(slope, bias_row)
    for r in range(16):
        piece = bias_row[0:1, r * HEAD_DIM : r * HEAD_DIM + HEAD_DIM]
        bias_parts[0, 16 + r : 17 + r, 0:HEAD_DIM] = piece
    column_sums(grads, bias_row)
    for r in range(12):
        piece = bias_row[0:1, r * HEAD_DIM : r * HEAD_DIM + HEAD_DIM]
        bias_parts[0, 4 + r : 5 + r, 0:HEAD_DIM] = piece
    for i in range(1, 16):
        bias_parts[i, 4:32, :] = bias_parts[0, 4:32, :]

    def stage_up(i):
        return cot_rows.at[i * 128 : i * 128 + 128, 0:1024]

    def stage_qkv(i):
        return here.probs3.at[pl.ds(0, 3), i * 128 : i * 128 + 128, :]

    claim(1)

    def up_share(core):
        for dx in ORDER:
            row_share(up_sum, here.hidden_t, slope, columns_of, stage_up, dx, core)

    def qkv_share(core):
        for dx in ORDER:
            row_share(qkv_sum, here.hidden_t, grads, layer_of, stage_qkv, dx, core)

    up_share(1)
    second.step1()
    second.send_half()
    up_share(0)
    qkv_share(1)
    second.step2()
    second.step3()
    qkv_share(0)
    up_sum.step2()
    small_reduce(bias_sum, bias_parts)
    qkv_sum.step2()
    bias_sum.step2()
    up_sum.step3()
    finish_outputs(first.step4(), here.tokens_here, vectors, outputs)
    leave(0)
    down_sum.step4()
    out_sum.step4()
    leave(4, 5)
    qkv_sum.step3()
    bias_sum.step3()
    finish_norm(
        second.step4(), here.tokens_here, here.cotangent_here, vectors, input_grad, here.norm_sums
    )
    leave(1)
    for i in range(16):
        here.norm_parts[i, :, :] = here.norm_sums[:, 128 * i : 128 * i + 128]
    norm_recv, norm_own, norm_full = here.norm_recv, here.norm_own, here.norm_full
    norm_sum = Direct(place, copies, place.along_dp, lambda i: norm_recv.at[i], direct_sems.at[1])
    for i in range(15):
        norm_sum.push(here.norm_parts.at[lax.rem(place.dp + i + 1, 16)], norm_recv.at[i], i)
    up_sum.step4()
    leave(3)
    norm_sum.wait_all()
    norm_own[...] = jnp.sum(norm_recv[...], 0) + here.norm_parts[place.dp]
    norm_all = Direct(place, copies, place.along_mp, lambda i: norm_full.at[i], direct_sems.at[2])
    for i in range(7):
        norm_all.push(norm_own, norm_full.at[i], i)
    qkv_sum.step4()
    bias_sum.step4()
    leave(2, 6)
    norm_all.wait_all()
    total = norm_own[...] + jnp.sum(norm_full[...], 0)
    norm_grad[...] = pltpu.roll(total, (128 - 16 * place.mp) % 128, 1)
    leave(7)
    copies.finish()
    for copy in leaving:
        copy.wait()


def layer(tokens, cotangent, weights, vectors, segments):
    anywhere = pl.BlockSpec(memory_space=pl.ANY)
    return pl.pallas_call(
        layer_kernel,
        out_shape=[jax.ShapeDtypeStruct(*spec) for spec in RESULTS.values()],
        in_specs=[anywhere] * 12,
        out_specs=[anywhere] * len(RESULTS),
        scratch_shapes=[pltpu.VMEM(*spec) for spec in (*SCRATCH.values(), *RESULTS.values())]
        + [
            pltpu.SMEM((1, 1024), jnp.int32),
            pltpu.SemaphoreType.DMA((2 * 8 + 4 * 15 + 2 * 10 + 5 * 15 + 37,)),
            pltpu.SemaphoreType.DMA((2, 8)),
            pltpu.SemaphoreType.DMA((4, 15)),
            pltpu.SemaphoreType.DMA((5, 15)),
            pltpu.SemaphoreType.DMA((2, 10)),
            pltpu.SemaphoreType.DMA((3, 15)),
            pltpu.SemaphoreType.DMA((23,)),
            pltpu.SemaphoreType.REGULAR((2,)),
        ],
        compiler_params=pltpu.CompilerParams(
            collective_id=1, has_side_effects=True, vmem_limit_bytes=63 * 2**20
        ),
        name="layer",
    )(tokens, cotangent, *weights, *vectors, segments)


def hand_over_kernel(*refs):
    large, small, large_out = refs[:6], refs[6:8], refs[8:14]
    qkv_bias, up_bias, out_bias, gain, shift, sems = refs[14:]
    moves = [
        pltpu.make_async_copy(src, dst, sems.at[i]) for i, (src, dst) in enumerate(zip(large, large_out))
    ]
    for move in moves:
        move.start()
    bias, norm = small
    dp = lax.axis_index("dp")
    out_bias[...] = bias[0:1, :]
    gain[...] = norm[0:1, 0:16]
    shift[...] = norm[1:2, 0:16]
    mine = pltpu.roll(bias[...], (128 - 4 * dp) % 128, 1)
    for c in range(3):
        qkv_bias[c] = mine[4 + 4 * c : 8 + 4 * c, 0:4]
    up_bias[...] = mine[16:32, :].T[0:4, :]
    for move in moves:
        move.wait()


def hand_over(results):
    anywhere = pl.BlockSpec(memory_space=pl.ANY)
    vmem = pl.BlockSpec(memory_space=pltpu.VMEM)
    small = [(3, 4, 4), (4, 16), (1, 128), (1, 16), (1, 16)]
    return pl.pallas_call(
        hand_over_kernel,
        out_shape=[jax.ShapeDtypeStruct(r.shape, r.dtype) for r in results[:6]]
        + [jax.ShapeDtypeStruct(shape, F32) for shape in small],
        in_specs=[vmem] * 8,
        out_specs=[anywhere] * 6 + [vmem] * 5,
        scratch_shapes=[pltpu.SemaphoreType.DMA((6,))],
        name="hand_over",
    )(*results)


def on_device(
    tokens,
    segments,
    norm_gain,
    norm_shift,
    qkv_weight,
    qkv_bias,
    up_weight,
    up_bias,
    out_weight,
    down_weight,
    out_bias,
    cotangent,
):
    results = layer(
        tokens,
        cotangent,
        (qkv_weight.transpose(1, 0, 2), up_weight, out_weight, down_weight),
        (norm_gain[None], norm_shift[None], out_bias[None], qkv_bias, up_bias.T),
        segments,
    )
    outputs, input_grad, qkv, up, out, down, qkv_b, up_b, out_b, gain, shift = hand_over(results)
    return (
        outputs,
        input_grad,
        gain[0],
        shift[0],
        qkv.transpose(1, 0, 2),
        qkv_b,
        up,
        up_b.T,
        out,
        down,
        out_b[0],
    )


def solution(mesh):
    return jax.shard_map(
        on_device,
        mesh=mesh,
        in_specs=(
            P(("dp", "mp"), None),
            P("dp", None),
            P("dp"),
            P("dp"),
            P("dp", None, "mp"),
            P(None, "mp", "dp"),
            P("dp", "mp"),
            P("mp", "dp"),
            P("mp", "dp"),
            P("mp", "dp"),
            P("dp"),
            P(("dp", "mp"), None),
        ),
        out_specs=(
            P(("dp", "mp"), None),
            P(("dp", "mp"), None),
            P(("dp", "mp")),
            P(("dp", "mp")),
            P("dp", None, "mp"),
            P(None, "mp", "dp"),
            P("dp", "mp"),
            P("mp", "dp"),
            P("mp", "dp"),
            P("mp", "dp"),
            P("dp"),
        ),
        check_vma=False,
    )
```
